32 devices in a mesh: space: 8 (over y, x, core), angle: 4 (over z).
Axes of the slice: x: 2, y: 2, z: 4, core: 2. Of those that a mesh axis runs over, the one named last changes fastest.
Arguments:
- phase_delay: float32 [2, 256, 2048], P(None, 'space'), may hold values from -6 to 6
- measured: float32 [4, 2, 256, 2048], P('angle', None, 'space'), may hold values from -6 to 6
- tilts: float32 [4, 2], P('angle'), may hold values from -0.4 to 0.4
- fresnel_taps: float32 [2, 2, 33], replicated, may hold values from -0.75 to 0.75
Outputs:
- gradient: float32 [2, 256, 2048], P(None, 'space', 'angle')
The draws below stay inside these ranges and needn't reach their ends.
All inputs are finite; a program needn't handle non-finite values.
Results may differ from the reference program's by a relative error of at most 0.0003.
Values sent between devices are 32-bit elements; how exact they have to be, the bound alone decides.
A program may use at most 64 MiB of HBM per device.

```python
import jax
import jax.numpy as jnp
from jax import lax

NY = 2048
TAPS = 33
SLICES = 2
NX = 256
ANGLES = 4


def steps_of(stream_key, extent, shards, least, largest):
    level = 1.0
    for axis_at, shards_of in shards:
        steps = jax.random.uniform(jax.random.fold_in(jax.random.fold_in(stream_key, 6), axis_at), (shards_of,), jnp.float32, least / len(shards), largest / len(shards))
        level = level * jnp.repeat(jnp.exp(steps), extent[axis_at] // shards_of).reshape((-1,) + (1,) * (len(extent) - 1 - axis_at))
    return level


def noise(stream_key, shape, width, limit, split=(), kind=jnp.bfloat16):
    values = width * jax.random.normal(stream_key, shape, jnp.float32)
    if split:
        values = values * steps_of(stream_key, shape, split, -0.22, 0.18)
    return jnp.clip(values, -limit, limit).astype(kind)


def setup_inputs(seed: int = 0) -> dict:
    keys = jax.random.split(jax.random.key(seed), 5)
    return {
        "phase_delay": noise(keys[0], (SLICES, NX, NY), 1.0, 6.0, ((1, 8),), jnp.float32),
        "measured": noise(keys[1], (ANGLES, 2, NX, NY), 1.0, 6.0, ((0, 4), (2, 8)), jnp.float32),
        "tilts": jnp.clip(jax.random.uniform(keys[2], (ANGLES, 2), jnp.float32, -0.4, 0.4) * steps_of(keys[2], (ANGLES, 2), ((0, 4),), -0.4, 0.0), -0.4, 0.4),
        "fresnel_taps": noise(keys[3], (2, 2, TAPS), (2 * TAPS) ** -0.5, 0.75, (), jnp.float32),
    }


def adjoint_kernel(kernel):
    return jnp.stack([kernel[0, ::-1], -kernel[1, ::-1]])


def along_rows(wave_field, kernel):
    reach = (kernel.shape[1] - 1) // 2
    length = wave_field.shape[1]
    padded = jnp.pad(wave_field, ((0, 0), (reach, reach), (0, 0)))
    real_part = jnp.zeros(wave_field.shape[1:], jnp.float32)
    imag_part = jnp.zeros(wave_field.shape[1:], jnp.float32)
    for offset in range(-reach, reach + 1):
        window = padded[:, reach - offset:reach - offset + length, :]
        tap_real = kernel[0, offset + reach]
        tap_imag = kernel[1, offset + reach]
        real_part = real_part + tap_real * window[0] - tap_imag * window[1]
        imag_part = imag_part + tap_real * window[1] + tap_imag * window[0]
    return jnp.stack([real_part, imag_part])


def along_columns(wave_field, kernel):
    reach = (kernel.shape[1] - 1) // 2
    length = wave_field.shape[2]
    padded = jnp.pad(wave_field, ((0, 0), (0, 0), (reach, reach)))
    real_part = jnp.zeros(wave_field.shape[1:], jnp.float32)
    imag_part = jnp.zeros(wave_field.shape[1:], jnp.float32)
    for offset in range(-reach, reach + 1):
        window = padded[:, :, reach - offset:reach - offset + length]
        tap_real = kernel[0, offset + reach]
        tap_imag = kernel[1, offset + reach]
        real_part = real_part + tap_real * window[0] - tap_imag * window[1]
        imag_part = imag_part + tap_real * window[1] + tap_imag * window[0]
    return jnp.stack([real_part, imag_part])


def transmit(wave_field, cosine, sine):
    return jnp.stack([cosine * wave_field[0] - sine * wave_field[1], cosine * wave_field[1] + sine * wave_field[0]])


def release(wave_field, cosine, sine):
    return jnp.stack([cosine * wave_field[0] + sine * wave_field[1], cosine * wave_field[1] - sine * wave_field[0]])


def reference(phase_delay, measured, tilts, fresnel_taps):
    row_taps = fresnel_taps[0]
    column_taps = fresnel_taps[1]
    row_back = adjoint_kernel(row_taps)
    column_back = adjoint_kernel(column_taps)
    cosines = jnp.cos(phase_delay)
    sines = jnp.sin(phase_delay)
    positions = jnp.arange(NX, dtype=jnp.float32)[:, None]
    columns = jnp.arange(NY, dtype=jnp.float32)[None, :]

    def one_angle(total, inputs):
        target, tilt = inputs
        ramp = tilt[0] * positions + tilt[1] * columns
        wave_field = jnp.stack([jnp.cos(ramp), jnp.sin(ramp)])
        stored = []
        for layer in range(SLICES):
            transmitted = transmit(wave_field, cosines[layer], sines[layer])
            stored.append(transmitted)
            wave_field = along_columns(along_rows(transmitted, row_taps), column_taps)
        backward = wave_field - target
        terms = [None] * SLICES
        for layer in reversed(range(SLICES)):
            sensitivity = along_rows(along_columns(backward, column_back), row_back)
            transmitted = stored[layer]
            terms[layer] = transmitted[0] * sensitivity[1] - transmitted[1] * sensitivity[0]
            backward = release(sensitivity, cosines[layer], sines[layer])
        return total + jnp.stack(terms), None

    total, unused = lax.scan(one_angle, jnp.zeros((SLICES, NX, NY), jnp.float32), (measured, tilts))
    return total
```

```python
import functools

import jax
import jax.numpy as jnp
from jax import lax
from jax.experimental import pallas as pl
from jax.experimental.pallas import tpu as pltpu
from jax.sharding import PartitionSpec as P

LANES = 128
MESH = pl.DeviceIdType.MESH
f32 = jnp.float32
bf16 = jnp.bfloat16


def sincos(x):
    k = jnp.floor(x * f32(0.3183098861837907) + f32(0.5))
    r = ((x - k * f32(3.140625)) - k * f32(9.67502593994140625e-4)) - k * f32(1.509957990978376e-7)
    sign = f32(1.0) - f32(2.0) * (k - f32(2.0) * jnp.floor(k * f32(0.5)))
    z = r * r
    s = f32(-2.5052108e-8)
    for c in (2.7557319e-6, -1.9841270e-4, 8.3333333e-3, -1.6666667e-1, 1.0):
        s = s * z + f32(c)
    c_ = f32(2.0876757e-9)
    for c in (-2.7557319e-7, 2.4801587e-5, -1.3888889e-3, 4.1666667e-2, -0.5, 1.0):
        c_ = c_ * z + f32(c)
    return sign * s * r, sign * c_


def split(x):
    hi = x.astype(bf16)
    return hi, (x - hi.astype(f32)).astype(bf16)


def kernel(
    sizes, phase, meas, tilts, taps, out,
    p0h, p1h, erow, ecol, t1s, w0s, w1s, zah, zal, zbh, zbl, zch, zcl, zdh, zdl,
    wf, wb, rf64, rf32, rb64, rb32, lam, lamh, gs, rsr,
    p0_send, p0_recv, p1_send, p1_recv, l_send, l_recv, g_send, g_recv,
):
    n_space, n_angle, chunks = sizes
    rows, cols = phase.shape[1], phase.shape[2]
    n_taps = taps.shape[2]
    reach = (n_taps - 1) // 2
    wide = rows + 2 * reach
    widest = rows + 4 * reach
    blocks = cols // LANES
    per = blocks // chunks
    piece = blocks // n_angle
    pieces_per_chunk = n_angle // chunks
    width = per * LANES
    s = lax.axis_index("space")
    q = lax.axis_index("angle")
    has_up = s > 0
    has_dn = s < n_space - 1
    up_id = (jnp.maximum(s - 1, 0), q)
    dn_id = (jnp.minimum(s + 1, n_space - 1), q)

    barrier = pltpu.get_barrier_semaphore()

    @pl.when(has_up)
    def _():
        pl.semaphore_signal(barrier, inc=1, device_id=up_id, device_id_type=MESH)

    @pl.when(has_dn)
    def _():
        pl.semaphore_signal(barrier, inc=1, device_id=dn_id, device_id_type=MESH)

    for j in range(n_angle):
        @pl.when(q != j)
        def _():
            pl.semaphore_signal(barrier, inc=1, device_id=(s, jnp.int32(j)), device_id_type=MESH)

    expected = n_angle - 1 + jnp.where(has_up, 1, 0) + jnp.where(has_dn, 1, 0)
    pl.semaphore_wait(barrier, expected)

    def p0_copy(side, c):
        at = pl.ds(c * width, width)
        return pltpu.make_async_remote_copy(
            phase.at[0, :, at], p0h.at[side, :, at], p0_send.at[side, c], p0_recv.at[side, c],
            device_id=dn_id if side == 0 else up_id, device_id_type=MESH)

    def p1_copy(side, c):
        at = pl.ds(c * width, width)
        first = rows - reach if side == 0 else 0
        return pltpu.make_async_remote_copy(
            phase.at[1, pl.ds(first, reach), at], p1h.at[side, :, at], p1_send.at[side, c], p1_recv.at[side, c],
            device_id=dn_id if side == 0 else up_id, device_id_type=MESH)

    def l_copy(side, c):
        at = pl.ds(c * per, per)
        return pltpu.make_async_remote_copy(
            lam.at[at], lamh.at[side, at], l_send.at[side, c], l_recv.at[side, c],
            device_id=dn_id if side == 0 else up_id, device_id_type=MESH)

    def g_copy(k, p):
        return pltpu.make_async_remote_copy(
            gs.at[k, pl.ds(p * piece, piece)], rsr.at[q, k], g_send.at[k, p], g_recv.at[k, q],
            device_id=(s, jnp.int32(p)), device_id_type=MESH)

    def g_arrival(k, j):
        return pltpu.make_async_remote_copy(
            gs.at[k, pl.ds(0, piece)], rsr.at[j, k], g_send.at[k, 0], g_recv.at[k, j],
            device_id=(s, jnp.int32(j)), device_id_type=MESH)

    def sending(make):
        @pl.when(has_dn)
        def _():
            make(0).start()

        @pl.when(has_up)
        def _():
            make(1).start()

    def arriving(make):
        @pl.when(has_up)
        def _():
            make(0).wait_recv()

        @pl.when(has_dn)
        def _():
            make(1).wait_recv()

    def sent(make):
        @pl.when(has_dn)
        def _():
            make(0).wait_send()

        @pl.when(has_up)
        def _():
            make(1).wait_send()

    for c in range(chunks):
        sending(lambda side: p0_copy(side, c))
        sending(lambda side: p1_copy(side, c))

    @pl.when(jnp.logical_not(has_up))
    def _():
        p0h[0] = jnp.zeros(p0h.shape[1:], f32)
        p1h[0] = jnp.zeros(p1h.shape[1:], f32)
        lamh[0] = jnp.zeros(lamh.shape[1:], f32)

    @pl.when(jnp.logical_not(has_dn))
    def _():
        p0h[1] = jnp.zeros(p0h.shape[1:], f32)
        p1h[1] = jnp.zeros(p1h.shape[1:], f32)
        lamh[1] = jnp.zeros(lamh.shape[1:], f32)

    for ref in (zah, zal, zbh, zbl, zch, zcl, zdh, zdl):
        ref[0] = jnp.zeros(ref.shape[1:], bf16)
        ref[blocks + 1] = jnp.zeros(ref.shape[1:], bf16)

    src = lax.broadcasted_iota(jnp.int32, (LANES, LANES), 0)
    dst = lax.broadcasted_iota(jnp.int32, (LANES, LANES), 1)
    away = dst - src
    turn = jnp.bitwise_and(away + LANES, LANES - 1)
    r_out = lax.broadcasted_iota(jnp.int32, (wide, LANES), 0)
    r_in = lax.broadcasted_iota(jnp.int32, (wide, LANES), 1)
    r_away = r_out + reach - r_in

    def build(step, carry):
        cr, ci, br, bi, rr, ri, ar, ai = carry
        a = step - reach
        hr, hi = taps[1, 0, step], taps[1, 1, step]
        gr, gi = taps[0, 0, step], taps[0, 1, step]
        here = turn == jnp.bitwise_and(a + LANES, LANES - 1)
        there = turn == jnp.bitwise_and(LANES - a, LANES - 1)
        r_here = r_away == a
        r_there = r_away == -a
        return (
            jnp.where(here, hr, cr), jnp.where(here, hi, ci),
            jnp.where(there, hr, br), jnp.where(there, -hi, bi),
            jnp.where(r_here, gr, rr), jnp.where(r_here, gi, ri),
            jnp.where(r_there, gr, ar), jnp.where(r_there, -gi, ai),
        )

    zc = jnp.zeros((LANES, LANES), f32)
    zr = jnp.zeros((wide, LANES), f32)
    cr, ci, br, bi, rr, ri, ar, ai = lax.fori_loop(
        0, n_taps, build, (zc, zc, zc, zc, zr, zr, zr, zr))
    masks = (away <= reach - LANES, jnp.abs(away) <= reach, away >= LANES - reach)
    for table, real, imag in ((wf, cr, ci), (wb, br, bi)):
        for m, mask in enumerate(masks):
            re, im = jnp.where(mask, real, 0.0), jnp.where(mask, imag, 0.0)
            hi, lo = split(jnp.concatenate(
                [jnp.concatenate([re, im], axis=1), jnp.concatenate([-im, re], axis=1)], axis=0))
            table[pl.ds(256 * m, 256)] = hi
            table[pl.ds(256 * (m + 3), 256)] = hi
            table[pl.ds(256 * (m + 6), 256)] = lo
    for big, small, real, imag in ((rf64, rf32, rr, ri), (rb64, rb32, ar, ai)):
        rh, rl = split(real)
        ih, il = split(imag)
        big[...] = jnp.concatenate([rh, ih, rl, il], axis=0)[:, :widest]
        small[...] = jnp.concatenate([rh[:rows], ih[:rows], rl[:rows], il[:rows]], axis=0)[:, :wide]

    row_at = lax.broadcasted_iota(jnp.int32, (widest, LANES), 0)
    row_no = (s * rows - 2 * reach + row_at).astype(f32)
    es, ec = sincos(tilts[0, 0] * row_no)
    inside = jnp.where(row_at < 2 * reach, jnp.where(has_up, 1.0, 0.0),
                       jnp.where(row_at >= 2 * reach + rows, jnp.where(has_dn, 1.0, 0.0), 1.0)).astype(f32)
    erow[0] = ec * inside
    erow[1] = es * inside
    w_at = lax.broadcasted_iota(jnp.int32, (wide, LANES), 0)
    inside1 = jnp.where(w_at < reach, jnp.where(has_up, 1.0, 0.0),
                        jnp.where(w_at >= reach + rows, jnp.where(has_dn, 1.0, 0.0), 1.0)).astype(f32)
    col_no = (lax.broadcasted_iota(jnp.int32, (blocks, LANES), 0) * LANES
              + lax.broadcasted_iota(jnp.int32, (blocks, LANES), 1)).astype(f32)
    ys, yc = sincos(tilts[0, 1] * col_no)
    ecol[0] = yc
    ecol[1] = ys

    def rows_conv(fields, matrix, zh, zl, c):
        out_rows = matrix.shape[0] // 4
        x = jnp.concatenate([part for pair in fields for part in pair], axis=1)
        hi, lo = split(x)
        m = matrix[...]
        y = jnp.dot(m, hi, preferred_element_type=f32)
        y = y[:2 * out_rows] + y[2 * out_rows:] + jnp.dot(m[:2 * out_rows], lo, preferred_element_type=f32)
        for b in range(per):
            o = b * 2 * LANES
            re = y[:out_rows, o:o + LANES] - y[out_rows:, o + LANES:o + 2 * LANES]
            im = y[:out_rows, o + LANES:o + 2 * LANES] + y[out_rows:, o:o + LANES]
            h, l = split(jnp.concatenate([re, im], axis=1))
            zh[1 + c * per + b] = h
            zl[1 + c * per + b] = l

    def cols_conv(zh, zl, table, c):
        out_rows = zh.shape[1]
        parts = [z[pl.ds(c * per + m, per)].reshape(per * out_rows, 2 * LANES)
                 for z in (zh, zl) for m in range(3)]
        x = jnp.concatenate(parts + parts[:3], axis=1)
        y = jnp.dot(x, table[...], preferred_element_type=f32)
        y = y.reshape(per, out_rows, 2 * LANES)
        return [(y[b, :, :LANES], y[b, :, LANES:]) for b in range(per)]

    def forward_a(c):
        arriving(lambda side: p0_copy(side, c))
        arriving(lambda side: p1_copy(side, c))
        fields = []
        for b in range(per):
            n = c * per + b
            at = slice(n * LANES, (n + 1) * LANES)
            sn, cs = sincos(jnp.concatenate([p0h[0, :, at], phase[0, :, at], p0h[1, :, at]], axis=0))
            yc, ys = ecol[0, n:n + 1, :], ecol[1, n:n + 1, :]
            tr, ti = cs * yc - sn * ys, cs * ys + sn * yc
            ec, es = erow[0], erow[1]
            re, im = tr * ec - ti * es, tr * es + ti * ec
            w0s[n, :, :LANES] = re[2 * reach:2 * reach + rows]
            w0s[n, :, LANES:] = im[2 * reach:2 * reach + rows]
            fields.append((re, im))
            sn, cs = sincos(jnp.concatenate([p1h[0, :, at], phase[1, :, at], p1h[1, :, at]], axis=0))
            t1s[n, :, :LANES] = cs * inside1
            t1s[n, :, LANES:] = sn * inside1
        rows_conv(fields, rf64, zah, zal, c)

    def forward_b(c):
        fields = []
        for b, (re, im) in enumerate(cols_conv(zah, zal, wf, c)):
            n = c * per + b
            cs, sn = t1s[n, :, :LANES], t1s[n, :, LANES:]
            wr, wi = cs * re - sn * im, cs * im + sn * re
            w1s[n, :, :LANES] = wr[reach:reach + rows]
            w1s[n, :, LANES:] = wi[reach:reach + rows]
            fields.append((wr, wi))
        rows_conv(fields, rf32, zbh, zbl, c)

    def forward_c(c):
        for b, (re, im) in enumerate(cols_conv(zbh, zbl, wf, c)):
            n = c * per + b
            at = slice(n * LANES, (n + 1) * LANES)
            lam[n, :, :LANES] = re - meas[0, 0, :, at]
            lam[n, :, LANES:] = im - meas[0, 1, :, at]
        sending(lambda side: l_copy(side, c))

    def backward_a(c):
        arriving(lambda side: l_copy(side, c))
        fields = []
        for b in range(per):
            n = c * per + b
            x = jnp.concatenate([lamh[0, n], lam[n], lamh[1, n]], axis=0)
            fields.append((x[:, :LANES], x[:, LANES:]))
        rows_conv(fields, rb64, zch, zcl, c)

    def send_terms(k, c):
        for p in range(c * pieces_per_chunk, (c + 1) * pieces_per_chunk):
            @pl.when(q != p)
            def _():
                g_copy(k, p).start()

            @pl.when(q == p)
            def _():
                rsr[q, k] = gs[k, p * piece:(p + 1) * piece]

    def backward_b(c):
        fields = []
        for b, (re, im) in enumerate(cols_conv(zch, zcl, wb, c)):
            n = c * per + b
            own = slice(reach, reach + rows)
            gs[1, n] = w1s[n, :, :LANES] * im[own] - w1s[n, :, LANES:] * re[own]
            cs, sn = t1s[n, :, :LANES], t1s[n, :, LANES:]
            fields.append((cs * re + sn * im, cs * im - sn * re))
        send_terms(1, c)
        rows_conv(fields, rb32, zdh, zdl, c)

    def backward_c(c):
        for b, (re, im) in enumerate(cols_conv(zdh, zdl, wb, c)):
            n = c * per + b
            gs[0, n] = w0s[n, :, :LANES] * im - w0s[n, :, LANES:] * re
        send_terms(0, c)

    for stages in ((forward_a, forward_b, forward_c), (backward_a, backward_b, backward_c)):
        for step in range(chunks + 2):
            for lag, stage in enumerate(stages):
                if 0 <= step - lag < chunks:
                    stage(step - lag)

    for k in (1, 0):
        for j in range(n_angle):
            @pl.when(q != j)
            def _():
                g_arrival(k, j).wait_recv()
        total = rsr[0, k]
        for j in range(1, n_angle):
            total = total + rsr[j, k]
        for b in range(piece):
            out[k, :, b * LANES:(b + 1) * LANES] = total[b]

    for c in range(chunks):
        sent(lambda side: p0_copy(side, c))
        sent(lambda side: p1_copy(side, c))
        sent(lambda side: l_copy(side, c))
    for k in (0, 1):
        for p in range(n_angle):
            @pl.when(q != p)
            def _():
                g_copy(k, p).wait_send()


def body(n_space, n_angle, phase_delay, measured, tilts, fresnel_taps):
    slices, rows, cols = phase_delay.shape
    reach = (fresnel_taps.shape[2] - 1) // 2
    blocks = cols // LANES
    chunks = 4
    wide, widest = rows + 2 * reach, rows + 4 * reach
    piece = blocks // n_angle
    vmem = pltpu.VMEM
    dma = pltpu.SemaphoreType.DMA
    scratch = [
        vmem((2, rows, cols), f32), vmem((2, reach, cols), f32),
        vmem((2, widest, LANES), f32), vmem((2, blocks, LANES), f32),
        vmem((blocks, wide, 2 * LANES), f32),
        vmem((blocks, rows, 2 * LANES), f32), vmem((blocks, rows, 2 * LANES), f32),
    ]
    for height in (wide, rows, wide, rows):
        scratch += [vmem((blocks + 2, height, 2 * LANES), bf16)] * 2
    scratch += [
        vmem((9 * 256, 256), bf16), vmem((9 * 256, 256), bf16),
        vmem((4 * wide, widest), bf16), vmem((4 * rows, wide), bf16),
        vmem((4 * wide, widest), bf16), vmem((4 * rows, wide), bf16),
        vmem((blocks, rows, 2 * LANES), f32), vmem((2, blocks, rows, 2 * LANES), f32),
        vmem((2, blocks, rows, LANES), f32), vmem((n_angle, 2, piece, rows, LANES), f32),
    ]
    scratch += [dma((2, chunks))] * 6 + [dma((2, n_angle))] * 2
    in_vmem = pl.BlockSpec(memory_space=pltpu.VMEM)
    in_smem = pl.BlockSpec(memory_space=pltpu.SMEM)
    return pl.pallas_call(
        functools.partial(kernel, (n_space, n_angle, chunks)),
        out_shape=jax.ShapeDtypeStruct((slices, rows, cols // n_angle), f32),
        in_specs=[in_vmem, in_vmem, in_smem, in_smem],
        out_specs=in_vmem,
        scratch_shapes=scratch,
        compiler_params=pltpu.CompilerParams(
            collective_id=0, has_side_effects=True, vmem_limit_bytes=48 * 1024 * 1024),
    )(phase_delay, measured, tilts, fresnel_taps)


def solution(mesh):
    return jax.shard_map(
        functools.partial(body, mesh.shape["space"], mesh.shape["angle"]),
        mesh=mesh,
        in_specs=(P(None, "space", None), P("angle", None, "space", None), P("angle", None), P()),
        out_specs=P(None, "space", "angle"),
        check_vma=False,
    )
```

```python
import functools

import jax
import jax.numpy as jnp
from jax import lax
from jax.experimental import pallas as pl
from jax.experimental.pallas import tpu as pltpu
from jax.sharding import PartitionSpec as P

LANES = 128
MESH = pl.DeviceIdType.MESH
f32 = jnp.float32
bf16 = jnp.bfloat16


def sincos(x):
    k = jnp.floor(x * f32(0.3183098861837907) + f32(0.5))
    r = ((x - k * f32(3.140625)) - k * f32(9.67502593994140625e-4)) - k * f32(1.509957990978376e-7)
    sign = f32(1.0) - f32(2.0) * (k - f32(2.0) * jnp.floor(k * f32(0.5)))
    z = r * r
    s = f32(-2.5052108e-8)
    for c in (2.7557319e-6, -1.9841270e-4, 8.3333333e-3, -1.6666667e-1, 1.0):
        s = s * z + f32(c)
    c_ = f32(2.0876757e-9)
    for c in (-2.7557319e-7, 2.4801587e-5, -1.3888889e-3, 4.1666667e-2, -0.5, 1.0):
        c_ = c_ * z + f32(c)
    return sign * s * r, sign * c_


def split(x):
    hi = x.astype(bf16)
    return hi, (x - hi.astype(f32)).astype(bf16)


def kernel(
    sizes, phase_in, meas_in, tilts_in, taps_in, out, phase, meas, tilts, taps,
    p0h, p1h, erow, ecol, t1s, w0s, w1s, zah, zal, zbh, zbl, zch, zcl, zdh, zdl,
    wf, wb, rf64, rf32, rb64, rb32, lam, lamh, gs, rsr,
    p0_send, p0_recv, p1_send, p1_recv, l_send, l_recv, g_send, g_recv, load,
):
    n_space, n_angle, chunks = sizes
    rows, cols = phase.shape[1], phase.shape[2]
    n_taps = taps.shape[2]
    reach = (n_taps - 1) // 2
    wide = rows + 2 * reach
    widest = rows + 4 * reach
    blocks = cols // LANES
    per = blocks // chunks
    piece = blocks // n_angle
    pieces_per_chunk = n_angle // chunks
    width = per * LANES
    s = lax.axis_index("space")
    q = lax.axis_index("angle")
    has_up = s > 0
    has_dn = s < n_space - 1
    up_id = (jnp.maximum(s - 1, 0), q)
    dn_id = (jnp.minimum(s + 1, n_space - 1), q)

    loads = [pltpu.make_async_copy(a, b, load.at[i]) for i, (a, b) in enumerate(
        ((taps_in, taps), (tilts_in, tilts), (phase_in, phase), (meas_in, meas)))]
    for copy in loads:
        copy.start()

    barrier = pltpu.get_barrier_semaphore()

    @pl.when(has_up)
    def _():
        pl.semaphore_signal(barrier, inc=1, device_id=up_id, device_id_type=MESH)

    @pl.when(has_dn)
    def _():
        pl.semaphore_signal(barrier, inc=1, device_id=dn_id, device_id_type=MESH)

    for j in range(n_angle):
        @pl.when(q != j)
        def _():
            pl.semaphore_signal(barrier, inc=1, device_id=(s, jnp.int32(j)), device_id_type=MESH)

    expected = n_angle - 1 + jnp.where(has_up, 1, 0) + jnp.where(has_dn, 1, 0)
    pl.semaphore_wait(barrier, expected)

    def p0_copy(side, c):
        at = pl.ds(c * width, width)
        return pltpu.make_async_remote_copy(
            phase_in.at[0, :, at], p0h.at[side, :, at], p0_send.at[side, c], p0_recv.at[side, c],
            device_id=dn_id if side == 0 else up_id, device_id_type=MESH)

    def p1_copy(side, c):
        at = pl.ds(c * width, width)
        first = rows - reach if side == 0 else 0
        return pltpu.make_async_remote_copy(
            phase_in.at[1, pl.ds(first, reach), at], p1h.at[side, :, at], p1_send.at[side, c], p1_recv.at[side, c],
            device_id=dn_id if side == 0 else up_id, device_id_type=MESH)

    def l_copy(side, c):
        at = pl.ds(c * per, per)
        return pltpu.make_async_remote_copy(
            lam.at[at], lamh.at[side, at], l_send.at[side, c], l_recv.at[side, c],
            device_id=dn_id if side == 0 else up_id, device_id_type=MESH)

    def g_copy(k, p):
        return pltpu.make_async_remote_copy(
            gs.at[k, pl.ds(p * piece, piece)], rsr.at[q, k], g_send.at[k, p], g_recv.at[k, q],
            device_id=(s, jnp.int32(p)), device_id_type=MESH)

    def g_arrival(k, j):
        return pltpu.make_async_remote_copy(
            gs.at[k, pl.ds(0, piece)], rsr.at[j, k], g_send.at[k, 0], g_recv.at[k, j],
            device_id=(s, jnp.int32(j)), device_id_type=MESH)

    def sending(make):
        @pl.when(has_dn)
        def _():
            make(0).start()

        @pl.when(has_up)
        def _():
            make(1).start()

    def arriving(make):
        @pl.when(has_up)
        def _():
            make(0).wait_recv()

        @pl.when(has_dn)
        def _():
            make(1).wait_recv()

    def sent(make):
        @pl.when(has_dn)
        def _():
            make(0).wait_send()

        @pl.when(has_up)
        def _():
            make(1).wait_send()

    for c in range(chunks):
        sending(lambda side: p0_copy(side, c))
        sending(lambda side: p1_copy(side, c))

    @pl.when(jnp.logical_not(has_up))
    def _():
        p0h[0] = jnp.zeros(p0h.shape[1:], f32)
        p1h[0] = jnp.zeros(p1h.shape[1:], f32)
        lamh[0] = jnp.zeros(lamh.shape[1:], f32)

    @pl.when(jnp.logical_not(has_dn))
    def _():
        p0h[1] = jnp.zeros(p0h.shape[1:], f32)
        p1h[1] = jnp.zeros(p1h.shape[1:], f32)
        lamh[1] = jnp.zeros(lamh.shape[1:], f32)

    for ref in (zah, zal, zbh, zbl, zch, zcl, zdh, zdl):
        ref[0] = jnp.zeros(ref.shape[1:], bf16)
        ref[blocks + 1] = jnp.zeros(ref.shape[1:], bf16)

    loads[0].wait()
    src = lax.broadcasted_iota(jnp.int32, (LANES, LANES), 0)
    dst = lax.broadcasted_iota(jnp.int32, (LANES, LANES), 1)
    away = dst - src
    turn = jnp.bitwise_and(away + LANES, LANES - 1)
    r_out = lax.broadcasted_iota(jnp.int32, (wide, LANES), 0)
    r_in = lax.broadcasted_iota(jnp.int32, (wide, LANES), 1)
    r_away = r_out + reach - r_in

    def build(step, carry):
        cr, ci, br, bi, rr, ri, ar, ai = carry
        a = step - reach
        hr, hi = taps[1, 0, step], taps[1, 1, step]
        gr, gi = taps[0, 0, step], taps[0, 1, step]
        here = turn == jnp.bitwise_and(a + LANES, LANES - 1)
        there = turn == jnp.bitwise_and(LANES - a, LANES - 1)
        r_here = r_away == a
        r_there = r_away == -a
        return (
            jnp.where(here, hr, cr), jnp.where(here, hi, ci),
            jnp.where(there, hr, br), jnp.where(there, -hi, bi),
            jnp.where(r_here, gr, rr), jnp.where(r_here, gi, ri),
            jnp.where(r_there, gr, ar), jnp.where(r_there, -gi, ai),
        )

    zc = jnp.zeros((LANES, LANES), f32)
    zr = jnp.zeros((wide, LANES), f32)
    cr, ci, br, bi, rr, ri, ar, ai = lax.fori_loop(
        0, n_taps, build, (zc, zc, zc, zc, zr, zr, zr, zr))
    near = jnp.abs(away) <= reach
    masks = (near, jnp.abs(away) >= LANES - reach)
    for table, real, imag in ((wf, cr, ci), (wb, br, bi)):
        for m, mask in enumerate(masks):
            re, im = jnp.where(mask, real, 0.0), jnp.where(mask, imag, 0.0)
            hi, lo = split(jnp.concatenate(
                [jnp.concatenate([re, im], axis=1), jnp.concatenate([-im, re], axis=1)], axis=0))
            table[pl.ds(256 * m, 256)] = hi
            table[pl.ds(256 * (m + 2), 256)] = hi
            table[pl.ds(256 * (m + 4), 256)] = lo
    for big, small, real, imag in ((rf64, rf32, rr, ri), (rb64, rb32, ar, ai)):
        rh, rl = split(real)
        ih, il = split(imag)
        big[...] = jnp.concatenate([rh, ih, rl, il], axis=0)[:, :widest]
        small[...] = jnp.concatenate([rh[:rows], ih[:rows], rl[:rows], il[:rows]], axis=0)[:, :wide]

    loads[1].wait()
    row_at = lax.broadcasted_iota(jnp.int32, (widest, LANES), 0)
    row_no = (s * rows - 2 * reach + row_at).astype(f32)
    es, ec = sincos(tilts[0, 0] * row_no)
    inside = jnp.where(row_at < 2 * reach, jnp.where(has_up, 1.0, 0.0),
                       jnp.where(row_at >= 2 * reach + rows, jnp.where(has_dn, 1.0, 0.0), 1.0)).astype(f32)
    erow[0] = ec * inside
    erow[1] = es * inside
    w_at = lax.broadcasted_iota(jnp.int32, (wide, LANES), 0)
    inside1 = jnp.where(w_at < reach, jnp.where(has_up, 1.0, 0.0),
                        jnp.where(w_at >= reach + rows, jnp.where(has_dn, 1.0, 0.0), 1.0)).astype(f32)
    col_no = (lax.broadcasted_iota(jnp.int32, (blocks, LANES), 0) * LANES
              + lax.broadcasted_iota(jnp.int32, (blocks, LANES), 1)).astype(f32)
    ys, yc = sincos(tilts[0, 1] * col_no)
    ecol[0] = yc
    ecol[1] = ys

    def rows_conv(fields, matrix, zh, zl, c):
        out_rows = matrix.shape[0] // 4
        x = jnp.concatenate([part for pair in fields for part in pair], axis=1)
        hi, lo = split(x)
        m = matrix[...]
        y = jnp.dot(m, hi, preferred_element_type=f32)
        y = y[:2 * out_rows] + y[2 * out_rows:] + jnp.dot(m[:2 * out_rows], lo, preferred_element_type=f32)
        for b in range(per):
            o = b * 2 * LANES
            re = y[:out_rows, o:o + LANES] - y[out_rows:, o + LANES:o + 2 * LANES]
            im = y[:out_rows, o + LANES:o + 2 * LANES] + y[out_rows:, o:o + LANES]
            h, l = split(jnp.concatenate([re, im], axis=1))
            zh[1 + c * per + b] = h
            zl[1 + c * per + b] = l

    def cols_conv(zh, zl, table, c):
        out_rows = zh.shape[1]
        lane = lax.broadcasted_iota(jnp.int32, (per, out_rows, 2 * LANES), 2)
        after = jnp.bitwise_and(lane, LANES - 1) < LANES // 2
        parts = []
        for z in (zh, zl):
            parts.append(z[pl.ds(c * per + 1, per)])
            parts.append(jnp.where(after, z[pl.ds(c * per + 2, per)], z[pl.ds(c * per, per)]))
        parts = [part.reshape(per * out_rows, 2 * LANES) for part in parts]
        x = jnp.concatenate(parts + parts[:2], axis=1)
        y = jnp.dot(x, table[...], preferred_element_type=f32)
        y = y.reshape(per, out_rows, 2 * LANES)
        return [(y[b, :, :LANES], y[b, :, LANES:]) for b in range(per)]

    def forward_a(c):
        fields = []
        for b in range(per):
            n = c * per + b
            at = slice(n * LANES, (n + 1) * LANES)
            sn, cs = sincos(jnp.concatenate([p0h[0, :, at], phase[0, :, at], p0h[1, :, at]], axis=0))
            yc, ys = ecol[0, n:n + 1, :], ecol[1, n:n + 1, :]
            tr, ti = cs * yc - sn * ys, cs * ys + sn * yc
            ec, es = erow[0], erow[1]
            re, im = tr * ec - ti * es, tr * es + ti * ec
            w0s[n, :, :LANES] = re[2 * reach:2 * reach + rows]
            w0s[n, :, LANES:] = im[2 * reach:2 * reach + rows]
            fields.append((re, im))
            sn, cs = sincos(jnp.concatenate([p1h[0, :, at], phase[1, :, at], p1h[1, :, at]], axis=0))
            t1s[n, :, :LANES] = cs * inside1
            t1s[n, :, LANES:] = sn * inside1
        rows_conv(fields, rf64, zah, zal, c)

    def forward_b(c):
        fields = []
        for b, (re, im) in enumerate(cols_conv(zah, zal, wf, c)):
            n = c * per + b
            cs, sn = t1s[n, :, :LANES], t1s[n, :, LANES:]
            wr, wi = cs * re - sn * im, cs * im + sn * re
            w1s[n, :, :LANES] = wr[reach:reach + rows]
            w1s[n, :, LANES:] = wi[reach:reach + rows]
            fields.append((wr, wi))
        rows_conv(fields, rf32, zbh, zbl, c)

    def forward_c(c):
        for b, (re, im) in enumerate(cols_conv(zbh, zbl, wf, c)):
            n = c * per + b
            at = slice(n * LANES, (n + 1) * LANES)
            lam[n, :, :LANES] = re - meas[0, 0, :, at]
            lam[n, :, LANES:] = im - meas[0, 1, :, at]

    def backward_a(c):
        fields = []
        for b in range(per):
            n = c * per + b
            x = jnp.concatenate([lamh[0, n], lam[n], lamh[1, n]], axis=0)
            fields.append((x[:, :LANES], x[:, LANES:]))
        rows_conv(fields, rb64, zch, zcl, c)

    def send_terms(k, c):
        for p in range(c * pieces_per_chunk, (c + 1) * pieces_per_chunk):
            @pl.when(q != p)
            def _():
                g_copy(k, p).start()

            @pl.when(q == p)
            def _():
                rsr[q, k] = gs[k, p * piece:(p + 1) * piece]

    def backward_b(c):
        fields = []
        for b, (re, im) in enumerate(cols_conv(zch, zcl, wb, c)):
            n = c * per + b
            own = slice(reach, reach + rows)
            gs[1, n] = w1s[n, :, :LANES] * im[own] - w1s[n, :, LANES:] * re[own]
            cs, sn = t1s[n, :, :LANES], t1s[n, :, LANES:]
            fields.append((cs * re + sn * im, cs * im - sn * re))
        rows_conv(fields, rb32, zdh, zdl, c)

    def backward_c(c):
        for b, (re, im) in enumerate(cols_conv(zdh, zdl, wb, c)):
            n = c * per + b
            gs[0, n] = w0s[n, :, :LANES] * im - w0s[n, :, LANES:] * re

    loads[2].wait()
    for step in range(chunks + 2):
        if step < chunks:
            arriving(lambda side: p0_copy(side, step))
            arriving(lambda side: p1_copy(side, step))
            forward_a(step)
        if 0 <= step - 1 < chunks:
            forward_b(step - 1)
        if step == 2:
            loads[3].wait()
        if 0 <= step - 2:
            forward_c(step - 2)
            sending(lambda side: l_copy(side, step - 2))

    for step in range(chunks + 2):
        if step < chunks:
            arriving(lambda side: l_copy(side, step))
            backward_a(step)
        if 0 <= step - 1 < chunks:
            backward_b(step - 1)
        if 0 <= step - 2:
            backward_c(step - 2)
        if 0 <= step - 1 < chunks:
            send_terms(1, step - 1)
        if 0 <= step - 2:
            send_terms(0, step - 2)

    for k in (1, 0):
        for j in range(n_angle):
            @pl.when(q != j)
            def _():
                g_arrival(k, j).wait_recv()
        total = rsr[0, k]
        for j in range(1, n_angle):
            total = total + rsr[j, k]
        for b in range(piece):
            out[k, :, b * LANES:(b + 1) * LANES] = total[b]

    for c in range(chunks):
        sent(lambda side: p0_copy(side, c))
        sent(lambda side: p1_copy(side, c))
        sent(lambda side: l_copy(side, c))
    for k in (0, 1):
        for p in range(n_angle):
            @pl.when(q != p)
            def _():
                g_copy(k, p).wait_send()


def body(n_space, n_angle, phase_delay, measured, tilts, fresnel_taps):
    slices, rows, cols = phase_delay.shape
    reach = (fresnel_taps.shape[2] - 1) // 2
    blocks = cols // LANES
    chunks = 4
    wide, widest = rows + 2 * reach, rows + 4 * reach
    piece = blocks // n_angle
    vmem = pltpu.VMEM
    dma = pltpu.SemaphoreType.DMA
    scratch = [
        vmem((slices, rows, cols), f32), vmem((1, 2, rows, cols), f32),
        pltpu.SMEM(tilts.shape, f32), pltpu.SMEM(fresnel_taps.shape, f32),
        vmem((2, rows, cols), f32), vmem((2, reach, cols), f32),
        vmem((2, widest, LANES), f32), vmem((2, blocks, LANES), f32),
        vmem((blocks, wide, 2 * LANES), f32),
        vmem((blocks, rows, 2 * LANES), f32), vmem((blocks, rows, 2 * LANES), f32),
    ]
    for height in (wide, rows, wide, rows):
        scratch += [vmem((blocks + 2, height, 2 * LANES), bf16)] * 2
    scratch += [
        vmem((6 * 256, 256), bf16), vmem((6 * 256, 256), bf16),
        vmem((4 * wide, widest), bf16), vmem((4 * rows, wide), bf16),
        vmem((4 * wide, widest), bf16), vmem((4 * rows, wide), bf16),
        vmem((blocks, rows, 2 * LANES), f32), vmem((2, blocks, rows, 2 * LANES), f32),
        vmem((2, blocks, rows, LANES), f32), vmem((n_angle, 2, piece, rows, LANES), f32),
    ]
    scratch += [dma((2, chunks))] * 6 + [dma((2, n_angle))] * 2 + [dma((4,))]
    in_hbm = pl.BlockSpec(memory_space=pltpu.HBM)
    return pl.pallas_call(
        functools.partial(kernel, (n_space, n_angle, chunks)),
        out_shape=jax.ShapeDtypeStruct((slices, rows, cols // n_angle), f32),
        in_specs=[in_hbm] * 4,
        out_specs=pl.BlockSpec(memory_space=pltpu.VMEM),
        scratch_shapes=scratch,
        compiler_params=pltpu.CompilerParams(
            collective_id=0, has_side_effects=True, vmem_limit_bytes=48 * 1024 * 1024),
    )(phase_delay, measured, tilts, fresnel_taps)


def solution(mesh):
    return jax.shard_map(
        functools.partial(body, mesh.shape["space"], mesh.shape["angle"]),
        mesh=mesh,
        in_specs=(P(None, "space", None), P("angle", None, "space", None), P("angle", None), P()),
        out_specs=P(None, "space", "angle"),
        check_vma=False,
    )
```

```python
import functools

import jax
import jax.numpy as jnp
from jax import lax
from jax.experimental import pallas as pl
from jax.experimental.pallas import tpu as pltpu
from jax.sharding import PartitionSpec as P

LANES = 128
MESH = pl.DeviceIdType.MESH
f32 = jnp.float32
bf16 = jnp.bfloat16


def sincos(x):
    k = jnp.floor(x * f32(0.3183098861837907) + f32(0.5))
    r = ((x - k * f32(3.140625)) - k * f32(9.67502593994140625e-4)) - k * f32(1.509957990978376e-7)
    sign = f32(1.0) - f32(2.0) * (k - f32(2.0) * jnp.floor(k * f32(0.5)))
    z = r * r
    s = f32(-2.5052108e-8)
    for c in (2.7557319e-6, -1.9841270e-4, 8.3333333e-3, -1.6666667e-1, 1.0):
        s = s * z + f32(c)
    c_ = f32(2.0876757e-9)
    for c in (-2.7557319e-7, 2.4801587e-5, -1.3888889e-3, 4.1666667e-2, -0.5, 1.0):
        c_ = c_ * z + f32(c)
    return sign * s * r, sign * c_


def split(x):
    hi = x.astype(bf16)
    return hi, (x - hi.astype(f32)).astype(bf16)


def kernel(
    sizes, phase_in, meas_in, tilts_in, taps_in, out, phase, meas, tilts, taps,
    p0h, p1h, erow, ecol, t1s, w0s, w1s, zah, zal, zbh, zbl, zch, zcl, zdh, zdl,
    wf, wb, rf64, rf32, rb64, rb32, lam, lamh, gs, rsr,
    p0_send, p0_recv, p1_send, p1_recv, l_send, l_recv, g_send, g_recv, load,
):
    n_space, n_angle, chunks = sizes
    rows, cols = phase.shape[1], phase.shape[2]
    n_taps = taps.shape[2]
    reach = (n_taps - 1) // 2
    wide = rows + 2 * reach
    widest = rows + 4 * reach
    blocks = cols // LANES
    per = blocks // chunks
    piece = blocks // n_angle
    pieces_per_chunk = n_angle // chunks
    width = per * LANES
    s = lax.axis_index("space")
    q = lax.axis_index("angle")
    has_up = s > 0
    has_dn = s < n_space - 1
    up_id = (jnp.maximum(s - 1, 0), q)
    dn_id = (jnp.minimum(s + 1, n_space - 1), q)

    loads = [pltpu.make_async_copy(a, b, load.at[i]) for i, (a, b) in enumerate(
        ((taps_in, taps), (tilts_in, tilts), (phase_in, phase), (meas_in, meas)))]
    for copy in loads:
        copy.start()

    barrier = pltpu.get_barrier_semaphore()

    @pl.when(has_up)
    def _():
        pl.semaphore_signal(barrier, inc=1, device_id=up_id, device_id_type=MESH)

    @pl.when(has_dn)
    def _():
        pl.semaphore_signal(barrier, inc=1, device_id=dn_id, device_id_type=MESH)

    for j in range(n_angle):
        @pl.when(q != j)
        def _():
            pl.semaphore_signal(barrier, inc=1, device_id=(s, jnp.int32(j)), device_id_type=MESH)

    expected = n_angle - 1 + jnp.where(has_up, 1, 0) + jnp.where(has_dn, 1, 0)
    pl.semaphore_wait(barrier, expected)

    def p0_copy(side, c):
        at = pl.ds(c * width, width)
        return pltpu.make_async_remote_copy(
            phase_in.at[0, :, at], p0h.at[side, :, at], p0_send.at[side, c], p0_recv.at[side, c],
            device_id=dn_id if side == 0 else up_id, device_id_type=MESH)

    def p1_copy(side, c):
        at = pl.ds(c * width, width)
        first = rows - reach if side == 0 else 0
        return pltpu.make_async_remote_copy(
            phase_in.at[1, pl.ds(first, reach), at], p1h.at[side, :, at], p1_send.at[side, c], p1_recv.at[side, c],
            device_id=dn_id if side == 0 else up_id, device_id_type=MESH)

    def l_copy(side, c):
        at = pl.ds(c * per, per)
        return pltpu.make_async_remote_copy(
            lam.at[at], lamh.at[side, at], l_send.at[side, c], l_recv.at[side, c],
            device_id=dn_id if side == 0 else up_id, device_id_type=MESH)

    def g_copy(k, p):
        return pltpu.make_async_remote_copy(
            gs.at[k, pl.ds(p * piece, piece)], rsr.at[q, k], g_send.at[k, p], g_recv.at[k, q],
            device_id=(s, jnp.int32(p)), device_id_type=MESH)

    def g_arrival(k, j):
        return pltpu.make_async_remote_copy(
            gs.at[k, pl.ds(0, piece)], rsr.at[j, k], g_send.at[k, 0], g_recv.at[k, j],
            device_id=(s, jnp.int32(j)), device_id_type=MESH)

    def sending(make):
        @pl.when(has_dn)
        def _():
            make(0).start()

        @pl.when(has_up)
        def _():
            make(1).start()

    def arriving(make):
        @pl.when(has_up)
        def _():
            make(0).wait_recv()

        @pl.when(has_dn)
        def _():
            make(1).wait_recv()

    def sent(make):
        @pl.when(has_dn)
        def _():
            make(0).wait_send()

        @pl.when(has_up)
        def _():
            make(1).wait_send()

    for c in range(chunks):
        sending(lambda side: p0_copy(side, c))
        sending(lambda side: p1_copy(side, c))

    @pl.when(jnp.logical_not(has_up))
    def _():
        p0h[0] = jnp.zeros(p0h.shape[1:], f32)
        p1h[0] = jnp.zeros(p1h.shape[1:], f32)
        lamh[0] = jnp.zeros(lamh.shape[1:], f32)

    @pl.when(jnp.logical_not(has_dn))
    def _():
        p0h[1] = jnp.zeros(p0h.shape[1:], f32)
        p1h[1] = jnp.zeros(p1h.shape[1:], f32)
        lamh[1] = jnp.zeros(lamh.shape[1:], f32)

    for ref in (zah, zal, zbh, zbl, zch, zcl, zdh, zdl):
        ref[0] = jnp.zeros(ref.shape[1:], bf16)
        ref[blocks + 1] = jnp.zeros(ref.shape[1:], bf16)

    loads[0].wait()
    src = lax.broadcasted_iota(jnp.int32, (LANES, LANES), 0)
    dst = lax.broadcasted_iota(jnp.int32, (LANES, LANES), 1)
    away = dst - src
    turn = jnp.bitwise_and(away + LANES, LANES - 1)
    r_out = lax.broadcasted_iota(jnp.int32, (wide, LANES), 0)
    r_in = lax.broadcasted_iota(jnp.int32, (wide, LANES), 1)
    r_away = r_out + reach - r_in

    def build(step, carry):
        cr, ci, br, bi, rr, ri, ar, ai = carry
        a = step - reach
        hr, hi = taps[1, 0, step], taps[1, 1, step]
        gr, gi = taps[0, 0, step], taps[0, 1, step]
        here = turn == jnp.bitwise_and(a + LANES, LANES - 1)
        there = turn == jnp.bitwise_and(LANES - a, LANES - 1)
        r_here = r_away == a
        r_there = r_away == -a
        return (
            jnp.where(here, hr, cr), jnp.where(here, hi, ci),
            jnp.where(there, hr, br), jnp.where(there, -hi, bi),
            jnp.where(r_here, gr, rr), jnp.where(r_here, gi, ri),
            jnp.where(r_there, gr, ar), jnp.where(r_there, -gi, ai),
        )

    zc = jnp.zeros((LANES, LANES), f32)
    zr = jnp.zeros((wide, LANES), f32)
    cr, ci, br, bi, rr, ri, ar, ai = lax.fori_loop(
        0, n_taps, build, (zc, zc, zc, zc, zr, zr, zr, zr))
    near = jnp.abs(away) <= reach
    masks = (near, jnp.abs(away) >= LANES - reach)
    for table, real, imag in ((wf, cr, ci), (wb, br, bi)):
        for m, mask in enumerate(masks):
            re, im = jnp.where(mask, real, 0.0), jnp.where(mask, imag, 0.0)
            hi, lo = split(jnp.concatenate(
                [jnp.concatenate([re, im], axis=1), jnp.concatenate([-im, re], axis=1)], axis=0))
            table[pl.ds(256 * m, 256)] = hi
            table[pl.ds(256 * (m + 2), 256)] = hi
            table[pl.ds(256 * (m + 4), 256)] = lo
    for big, small, real, imag in ((rf64, rf32, rr, ri), (rb64, rb32, ar, ai)):
        rh, rl = split(real)
        ih, il = split(imag)
        big[...] = jnp.concatenate([rh, ih, rl, il], axis=0)[:, :widest]
        small[...] = jnp.concatenate([rh[:rows], ih[:rows], rl[:rows], il[:rows]], axis=0)[:, :wide]

    loads[1].wait()
    row_at = lax.broadcasted_iota(jnp.int32, (widest, LANES), 0)
    row_no = (s * rows - 2 * reach + row_at).astype(f32)
    es, ec = sincos(tilts[0, 0] * row_no)
    inside = jnp.where(row_at < 2 * reach, jnp.where(has_up, 1.0, 0.0),
                       jnp.where(row_at >= 2 * reach + rows, jnp.where(has_dn, 1.0, 0.0), 1.0)).astype(f32)
    erow[0] = ec * inside
    erow[1] = es * inside
    w_at = lax.broadcasted_iota(jnp.int32, (wide, LANES), 0)
    inside1 = jnp.where(w_at < reach, jnp.where(has_up, 1.0, 0.0),
                        jnp.where(w_at >= reach + rows, jnp.where(has_dn, 1.0, 0.0), 1.0)).astype(f32)
    col_no = (lax.broadcasted_iota(jnp.int32, (blocks, LANES), 0) * LANES
              + lax.broadcasted_iota(jnp.int32, (blocks, LANES), 1)).astype(f32)
    ys, yc = sincos(tilts[0, 1] * col_no)
    ecol[0] = yc
    ecol[1] = ys

    def rows_conv(fields, matrix, zh, zl, c):
        out_rows = matrix.shape[0] // 4
        x = jnp.concatenate([part for pair in fields for part in pair], axis=1)
        hi, lo = split(x)
        m = matrix[...]
        y = jnp.dot(m, hi, preferred_element_type=f32)
        y = y[:2 * out_rows] + y[2 * out_rows:] + jnp.dot(m[:2 * out_rows], lo, preferred_element_type=f32)
        for b in range(per):
            o = b * 2 * LANES
            re = y[:out_rows, o:o + LANES] - y[out_rows:, o + LANES:o + 2 * LANES]
            im = y[:out_rows, o + LANES:o + 2 * LANES] + y[out_rows:, o:o + LANES]
            h, l = split(jnp.concatenate([re, im], axis=1))
            zh[1 + c * per + b] = h
            zl[1 + c * per + b] = l

    def cols_conv(zh, zl, table, c):
        out_rows = zh.shape[1]
        lane = lax.broadcasted_iota(jnp.int32, (per, out_rows, 2 * LANES), 2)
        after = jnp.bitwise_and(lane, LANES - 1) < LANES // 2
        parts = []
        for z in (zh, zl):
            parts.append(z[pl.ds(c * per + 1, per)])
            parts.append(jnp.where(after, z[pl.ds(c * per + 2, per)], z[pl.ds(c * per, per)]))
        parts = [part.reshape(per * out_rows, 2 * LANES) for part in parts]
        x = jnp.concatenate(parts + parts[:2], axis=1)
        y = jnp.dot(x, table[...], preferred_element_type=f32)
        y = y.reshape(per, out_rows, 2 * LANES)
        return [(y[b, :, :LANES], y[b, :, LANES:]) for b in range(per)]

    def forward_a(c):
        fields = []
        for b in range(per):
            n = c * per + b
            at = slice(n * LANES, (n + 1) * LANES)
            sn, cs = sincos(jnp.concatenate([p0h[0, :, at], phase[0, :, at], p0h[1, :, at]], axis=0))
            yc, ys = ecol[0, n:n + 1, :], ecol[1, n:n + 1, :]
            tr, ti = cs * yc - sn * ys, cs * ys + sn * yc
            ec, es = erow[0], erow[1]
            re, im = tr * ec - ti * es, tr * es + ti * ec
            w0s[n, :, :LANES] = re[2 * reach:2 * reach + rows]
            w0s[n, :, LANES:] = im[2 * reach:2 * reach + rows]
            fields.append((re, im))
            sn, cs = sincos(jnp.concatenate([p1h[0, :, at], phase[1, :, at], p1h[1, :, at]], axis=0))
            t1s[n, :, :LANES] = cs * inside1
            t1s[n, :, LANES:] = sn * inside1
        rows_conv(fields, rf64, zah, zal, c)

    def forward_b(c):
        fields = []
        for b, (re, im) in enumerate(cols_conv(zah, zal, wf, c)):
            n = c * per + b
            cs, sn = t1s[n, :, :LANES], t1s[n, :, LANES:]
            wr, wi = cs * re - sn * im, cs * im + sn * re
            w1s[n, :, :LANES] = wr[reach:reach + rows]
            w1s[n, :, LANES:] = wi[reach:reach + rows]
            fields.append((wr, wi))
        rows_conv(fields, rf32, zbh, zbl, c)

    def forward_c(c):
        for b, (re, im) in enumerate(cols_conv(zbh, zbl, wf, c)):
            n = c * per + b
            at = slice(n * LANES, (n + 1) * LANES)
            lam[n, :, :LANES] = re - meas[0, 0, :, at]
            lam[n, :, LANES:] = im - meas[0, 1, :, at]

    def backward_a(c):
        fields = []
        for b in range(per):
            n = c * per + b
            x = jnp.concatenate([lamh[0, n], lam[n], lamh[1, n]], axis=0)
            fields.append((x[:, :LANES], x[:, LANES:]))
        rows_conv(fields, rb64, zch, zcl, c)

    def send_terms(k, c):
        for p in range(c * pieces_per_chunk, (c + 1) * pieces_per_chunk):
            @pl.when(q != p)
            def _():
                g_copy(k, p).start()

            @pl.when(q == p)
            def _():
                rsr[q, k] = gs[k, p * piece:(p + 1) * piece]

    def backward_b(c):
        fields = []
        for b, (re, im) in enumerate(cols_conv(zch, zcl, wb, c)):
            n = c * per + b
            own = slice(reach, reach + rows)
            gs[1, n] = w1s[n, :, :LANES] * im[own] - w1s[n, :, LANES:] * re[own]
            cs, sn = t1s[n, :, :LANES], t1s[n, :, LANES:]
            fields.append((cs * re + sn * im, cs * im - sn * re))
        rows_conv(fields, rb32, zdh, zdl, c)

    def backward_c(c):
        for b, (re, im) in enumerate(cols_conv(zdh, zdl, wb, c)):
            n = c * per + b
            gs[0, n] = w0s[n, :, :LANES] * im - w0s[n, :, LANES:] * re

    loads[2].wait()
    for step in range(chunks + 2):
        if step < chunks:
            arriving(lambda side: p0_copy(side, step))
            arriving(lambda side: p1_copy(side, step))
            forward_a(step)
        if 0 <= step - 1 < chunks:
            forward_b(step - 1)
        if step == 2:
            loads[3].wait()
        if 0 <= step - 2:
            forward_c(step - 2)
            sending(lambda side: l_copy(side, step - 2))

    for step in range(chunks + 2):
        if step < chunks:
            arriving(lambda side: l_copy(side, step))
            backward_a(step)
        if 0 <= step - 1 < chunks:
            backward_b(step - 1)
        if 0 <= step - 2:
            backward_c(step - 2)
        if 0 <= step - 1 < chunks:
            send_terms(1, step - 1)
        if 0 <= step - 2:
            send_terms(0, step - 2)

    for k in (1, 0):
        for j in range(n_angle):
            @pl.when(q != j)
            def _():
                g_arrival(k, j).wait_recv()
        total = rsr[0, k]
        for j in range(1, n_angle):
            total = total + rsr[j, k]
        for b in range(piece):
            out[k, :, b * LANES:(b + 1) * LANES] = total[b]

    for c in range(chunks):
        sent(lambda side: p0_copy(side, c))
        sent(lambda side: p1_copy(side, c))
        sent(lambda side: l_copy(side, c))
    for k in (0, 1):
        for p in range(n_angle):
            @pl.when(q != p)
            def _():
                g_copy(k, p).wait_send()


def body(n_space, n_angle, phase_delay, measured, tilts, fresnel_taps):
    slices, rows, cols = phase_delay.shape
    reach = (fresnel_taps.shape[2] - 1) // 2
    blocks = cols // LANES
    chunks = 4
    wide, widest = rows + 2 * reach, rows + 4 * reach
    piece = blocks // n_angle
    vmem = pltpu.VMEM
    dma = pltpu.SemaphoreType.DMA
    scratch = [
        vmem((slices, rows, cols), f32), vmem((1, 2, rows, cols), f32),
        pltpu.SMEM(tilts.shape, f32), pltpu.SMEM(fresnel_taps.shape, f32),
        vmem((2, rows, cols), f32), vmem((2, reach, cols), f32),
        vmem((2, widest, LANES), f32), vmem((2, blocks, LANES), f32),
        vmem((blocks, wide, 2 * LANES), f32),
        vmem((blocks, rows, 2 * LANES), f32), vmem((blocks, rows, 2 * LANES), f32),
    ]
    for height in (wide, rows, wide, rows):
        scratch += [vmem((blocks + 2, height, 2 * LANES), bf16)] * 2
    scratch += [
        vmem((6 * 256, 256), bf16), vmem((6 * 256, 256), bf16),
        vmem((4 * wide, widest), bf16), vmem((4 * rows, wide), bf16),
        vmem((4 * wide, widest), bf16), vmem((4 * rows, wide), bf16),
        vmem((blocks, rows, 2 * LANES), f32), vmem((2, blocks, rows, 2 * LANES), f32),
        vmem((2, blocks, rows, LANES), f32), vmem((n_angle, 2, piece, rows, LANES), f32),
    ]
    scratch += [dma((2, chunks))] * 6 + [dma((2, n_angle))] * 2 + [dma((4,))]
    in_hbm = pl.BlockSpec(memory_space=pltpu.HBM)
    return pl.pallas_call(
        functools.partial(kernel, (n_space, n_angle, chunks)),
        out_shape=jax.ShapeDtypeStruct((slices, rows, cols // n_angle), f32),
        in_specs=[in_hbm] * 4,
        out_specs=pl.BlockSpec(memory_space=pltpu.VMEM),
        scratch_shapes=scratch,
        compiler_params=pltpu.CompilerParams(
            collective_id=0, has_side_effects=True, vmem_limit_bytes=62 * 1024 * 1024),
    )(phase_delay, measured, tilts, fresnel_taps)


def solution(mesh):
    return jax.shard_map(
        functools.partial(body, mesh.shape["space"], mesh.shape["angle"]),
        mesh=mesh,
        in_specs=(P(None, "space", None), P("angle", None, "space", None), P("angle", None), P()),
        out_specs=P(None, "space", "angle"),
        check_vma=False,
    )
```

```python
import functools

import jax
import jax.numpy as jnp
from jax import lax
from jax.experimental import pallas as pl
from jax.experimental.pallas import tpu as pltpu
from jax.sharding import PartitionSpec as P

LANES = 128
MESH = pl.DeviceIdType.MESH
f32 = jnp.float32
bf16 = jnp.bfloat16


def sincos(x):
    k = jnp.floor(x * f32(0.3183098861837907) + f32(0.5))
    r = ((x - k * f32(3.140625)) - k * f32(9.67502593994140625e-4)) - k * f32(1.509957990978376e-7)
    sign = f32(1.0) - f32(2.0) * (k - f32(2.0) * jnp.floor(k * f32(0.5)))
    z = r * r
    s = f32(-2.5052108e-8)
    for c in (2.7557319e-6, -1.9841270e-4, 8.3333333e-3, -1.6666667e-1, 1.0):
        s = s * z + f32(c)
    c_ = f32(2.0876757e-9)
    for c in (-2.7557319e-7, 2.4801587e-5, -1.3888889e-3, 4.1666667e-2, -0.5, 1.0):
        c_ = c_ * z + f32(c)
    return sign * s * r, sign * c_


def split(x):
    hi = x.astype(bf16)
    return hi, (x - hi.astype(f32)).astype(bf16)


def kernel(
    sizes, phase_in, meas_in, tilts_in, taps_in, out, phase, meas, tilts, taps,
    p0h, p1h, erow, ecol, t1s, w0s, w1s, zah, zal, zbh, zbl, zch, zcl, zdh, zdl,
    wf, wb, rf64, rf32, rb64, rb32, lam, lamh, gs, rsr,
    p0_send, p0_recv, p1_send, p1_recv, l_send, l_recv, g_send, g_recv, load,
    held0, held1, heldl, ra_send, ra_recv, rb_send, rb_recv,
):
    n_space, n_angle, chunks = sizes
    rows, cols = phase.shape[1], phase.shape[2]
    n_taps = taps.shape[2]
    reach = (n_taps - 1) // 2
    wide = rows + 2 * reach
    widest = rows + 4 * reach
    blocks = cols // LANES
    per = blocks // chunks
    piece = blocks // n_angle
    pieces_per_chunk = n_angle // chunks
    width = per * LANES
    s = lax.axis_index("space")
    q = lax.axis_index("angle")
    has_up = s > 0
    has_dn = s < n_space - 1
    up_id = (jnp.maximum(s - 1, 0), q)
    dn_id = (jnp.minimum(s + 1, n_space - 1), q)

    loads = [pltpu.make_async_copy(a, b, load.at[i]) for i, (a, b) in enumerate(
        ((taps_in, taps), (tilts_in, tilts), (phase_in, phase), (meas_in, meas)))]
    for copy in loads:
        copy.start()

    relayed = n_space == 8
    mid = n_space // 2
    upper, lower = s == mid - 1, s == mid
    relays = (n_space - 1, 0)
    if relayed:
        from_up, from_dn = has_up & (s != mid), has_dn & (s != mid - 1)
    else:
        from_up, from_dn = has_up, has_dn

    barrier = pltpu.get_barrier_semaphore()
    if relayed:
        for strip in relays:
            @pl.when(upper | lower)
            def _():
                pl.semaphore_signal(barrier, inc=1, device_id=(jnp.int32(strip), q), device_id_type=MESH)

            @pl.when(s == strip)
            def _():
                for middle in (mid - 1, mid):
                    pl.semaphore_signal(barrier, inc=1, device_id=(jnp.int32(middle), q), device_id_type=MESH)

    @pl.when(has_up)
    def _():
        pl.semaphore_signal(barrier, inc=1, device_id=up_id, device_id_type=MESH)

    @pl.when(has_dn)
    def _():
        pl.semaphore_signal(barrier, inc=1, device_id=dn_id, device_id_type=MESH)

    for j in range(n_angle):
        @pl.when(q != j)
        def _():
            pl.semaphore_signal(barrier, inc=1, device_id=(s, jnp.int32(j)), device_id_type=MESH)

    expected = n_angle - 1 + jnp.where(has_up, 1, 0) + jnp.where(has_dn, 1, 0)
    if relayed:
        expected = expected + jnp.where(upper | lower | (s == 0) | (s == n_space - 1), 2, 0)
    pl.semaphore_wait(barrier, expected)

    def p0_copy(side, c):
        at = pl.ds(c * width, width)
        return pltpu.make_async_remote_copy(
            phase_in.at[0, :, at], p0h.at[side, :, at], p0_send.at[side, c], p0_recv.at[side, c],
            device_id=dn_id if side == 0 else up_id, device_id_type=MESH)

    def p1_copy(side, c):
        at = pl.ds(c * width, width)
        first = rows - reach if side == 0 else 0
        return pltpu.make_async_remote_copy(
            phase_in.at[1, pl.ds(first, reach), at], p1h.at[side, :, at], p1_send.at[side, c], p1_recv.at[side, c],
            device_id=dn_id if side == 0 else up_id, device_id_type=MESH)

    def l_copy(side, c):
        at = pl.ds(c * per, per)
        return pltpu.make_async_remote_copy(
            lam.at[at], lamh.at[side, at], l_send.at[side, c], l_recv.at[side, c],
            device_id=dn_id if side == 0 else up_id, device_id_type=MESH)

    def g_copy(k, p):
        return pltpu.make_async_remote_copy(
            gs.at[k, pl.ds(p * piece, piece)], rsr.at[q, k], g_send.at[k, p], g_recv.at[k, q],
            device_id=(s, jnp.int32(p)), device_id_type=MESH)

    def g_arrival(k, j):
        return pltpu.make_async_remote_copy(
            gs.at[k, pl.ds(0, piece)], rsr.at[j, k], g_send.at[k, 0], g_recv.at[k, j],
            device_id=(s, jnp.int32(j)), device_id_type=MESH)

    half = per // 2
    lanes = width // 2

    def parts_of(kind, d, h, c):
        if kind == 2:
            at, mine = pl.ds(c * per + h * half, half), pl.ds(c * half, half)
            return lam.at[at], heldl.at[d, mine], lamh.at[d, at]
        at, mine = pl.ds(c * width + h * lanes, lanes), pl.ds(c * lanes, lanes)
        if kind == 0:
            return phase_in.at[0, :, at], held0.at[d, :, mine], p0h.at[d, :, at]
        first = rows - reach if d == 0 else 0
        return phase_in.at[1, pl.ds(first, reach), at], held1.at[d, :, mine], p1h.at[d, :, at]

    def to_relay(kind, d, h, c):
        a, b, _ = parts_of(kind, d, h, c)
        return pltpu.make_async_remote_copy(
            a, b, ra_send.at[kind, h, c], ra_recv.at[kind, d, c],
            device_id=(jnp.int32(relays[h]), q), device_id_type=MESH)

    def from_relay(kind, d, h, c):
        _, b, e = parts_of(kind, d, h, c)
        return pltpu.make_async_remote_copy(
            b, e, rb_send.at[kind, d, c], rb_recv.at[kind, h, c],
            device_id=(jnp.int32(mid if d == 0 else mid - 1), q), device_id_type=MESH)

    def middle(d):
        return upper if d == 0 else lower

    def relay(kinds):
        if not relayed:
            return
        for h in range(2):
            @pl.when(s == relays[h])
            def _():
                for c in range(chunks):
                    for d in range(2):
                        for kind in kinds:
                            to_relay(kind, d, h, c).wait_recv()
                            from_relay(kind, d, h, c).start()

    def sending(make, kind, c):
        @pl.when(from_dn)
        def _():
            make(0).start()

        @pl.when(from_up)
        def _():
            make(1).start()

        if relayed:
            for d in range(2):
                @pl.when(middle(d))
                def _():
                    for h in range(2):
                        to_relay(kind, d, h, c).start()

    def arriving(make, kind, c):
        @pl.when(from_up)
        def _():
            make(0).wait_recv()

        @pl.when(from_dn)
        def _():
            make(1).wait_recv()

        if relayed:
            for d in range(2):
                @pl.when(middle(1 - d))
                def _():
                    for h in range(2):
                        from_relay(kind, d, h, c).wait_recv()

    def sent(make, kind, c):
        @pl.when(from_dn)
        def _():
            make(0).wait_send()

        @pl.when(from_up)
        def _():
            make(1).wait_send()

        if relayed:
            for d in range(2):
                @pl.when(middle(d))
                def _():
                    for h in range(2):
                        to_relay(kind, d, h, c).wait_send()
            for h in range(2):
                @pl.when(s == relays[h])
                def _():
                    for d in range(2):
                        from_relay(kind, d, h, c).wait_send()

    for c in range(chunks):
        sending(lambda side: p0_copy(side, c), 0, c)
        sending(lambda side: p1_copy(side, c), 1, c)

    @pl.when(jnp.logical_not(has_up))
    def _():
        p0h[0] = jnp.zeros(p0h.shape[1:], f32)
        p1h[0] = jnp.zeros(p1h.shape[1:], f32)
        lamh[0] = jnp.zeros(lamh.shape[1:], f32)

    @pl.when(jnp.logical_not(has_dn))
    def _():
        p0h[1] = jnp.zeros(p0h.shape[1:], f32)
        p1h[1] = jnp.zeros(p1h.shape[1:], f32)
        lamh[1] = jnp.zeros(lamh.shape[1:], f32)

    for ref in (zah, zal, zbh, zbl, zch, zcl, zdh, zdl):
        ref[0] = jnp.zeros(ref.shape[1:], bf16)
        ref[blocks + 1] = jnp.zeros(ref.shape[1:], bf16)

    loads[0].wait()
    src = lax.broadcasted_iota(jnp.int32, (LANES, LANES), 0)
    dst = lax.broadcasted_iota(jnp.int32, (LANES, LANES), 1)
    away = dst - src
    turn = jnp.bitwise_and(away + LANES, LANES - 1)
    r_out = lax.broadcasted_iota(jnp.int32, (wide, LANES), 0)
    r_in = lax.broadcasted_iota(jnp.int32, (wide, LANES), 1)
    r_away = r_out + reach - r_in

    def build(step, carry):
        cr, ci, br, bi, rr, ri, ar, ai = carry
        a = step - reach
        hr, hi = taps[1, 0, step], taps[1, 1, step]
        gr, gi = taps[0, 0, step], taps[0, 1, step]
        here = turn == jnp.bitwise_and(a + LANES, LANES - 1)
        there = turn == jnp.bitwise_and(LANES - a, LANES - 1)
        r_here = r_away == a
        r_there = r_away == -a
        return (
            jnp.where(here, hr, cr), jnp.where(here, hi, ci),
            jnp.where(there, hr, br), jnp.where(there, -hi, bi),
            jnp.where(r_here, gr, rr), jnp.where(r_here, gi, ri),
            jnp.where(r_there, gr, ar), jnp.where(r_there, -gi, ai),
        )

    zc = jnp.zeros((LANES, LANES), f32)
    zr = jnp.zeros((wide, LANES), f32)
    cr, ci, br, bi, rr, ri, ar, ai = lax.fori_loop(
        0, n_taps, build, (zc, zc, zc, zc, zr, zr, zr, zr))
    near = jnp.abs(away) <= reach
    masks = (near, jnp.abs(away) >= LANES - reach)
    for table, real, imag in ((wf, cr, ci), (wb, br, bi)):
        for m, mask in enumerate(masks):
            re, im = jnp.where(mask, real, 0.0), jnp.where(mask, imag, 0.0)
            hi, lo = split(jnp.concatenate(
                [jnp.concatenate([re, im], axis=1), jnp.concatenate([-im, re], axis=1)], axis=0))
            table[pl.ds(256 * m, 256)] = hi
            table[pl.ds(256 * (m + 2), 256)] = hi
            table[pl.ds(256 * (m + 4), 256)] = lo
    for big, small, real, imag in ((rf64, rf32, rr, ri), (rb64, rb32, ar, ai)):
        rh, rl = split(real)
        ih, il = split(imag)
        big[...] = jnp.concatenate([rh, ih, rl, il], axis=0)[:, :widest]
        small[...] = jnp.concatenate([rh[:rows], ih[:rows], rl[:rows], il[:rows]], axis=0)[:, :wide]

    loads[1].wait()
    row_at = lax.broadcasted_iota(jnp.int32, (widest, LANES), 0)
    row_no = (s * rows - 2 * reach + row_at).astype(f32)
    es, ec = sincos(tilts[0, 0] * row_no)
    inside = jnp.where(row_at < 2 * reach, jnp.where(has_up, 1.0, 0.0),
                       jnp.where(row_at >= 2 * reach + rows, jnp.where(has_dn, 1.0, 0.0), 1.0)).astype(f32)
    erow[0] = ec * inside
    erow[1] = es * inside
    w_at = lax.broadcasted_iota(jnp.int32, (wide, LANES), 0)
    inside1 = jnp.where(w_at < reach, jnp.where(has_up, 1.0, 0.0),
                        jnp.where(w_at >= reach + rows, jnp.where(has_dn, 1.0, 0.0), 1.0)).astype(f32)
    col_no = (lax.broadcasted_iota(jnp.int32, (blocks, LANES), 0) * LANES
              + lax.broadcasted_iota(jnp.int32, (blocks, LANES), 1)).astype(f32)
    ys, yc = sincos(tilts[0, 1] * col_no)
    ecol[0] = yc
    ecol[1] = ys

    def rows_conv(fields, matrix, zh, zl, c):
        out_rows = matrix.shape[0] // 4
        x = jnp.concatenate([part for pair in fields for part in pair], axis=1)
        hi, lo = split(x)
        m = matrix[...]
        y = jnp.dot(m, hi, preferred_element_type=f32)
        y = y[:2 * out_rows] + y[2 * out_rows:] + jnp.dot(m[:2 * out_rows], lo, preferred_element_type=f32)
        for b in range(per):
            o = b * 2 * LANES
            re = y[:out_rows, o:o + LANES] - y[out_rows:, o + LANES:o + 2 * LANES]
            im = y[:out_rows, o + LANES:o + 2 * LANES] + y[out_rows:, o:o + LANES]
            h, l = split(jnp.concatenate([re, im], axis=1))
            zh[1 + c * per + b] = h
            zl[1 + c * per + b] = l

    def cols_conv(zh, zl, table, c):
        out_rows = zh.shape[1]
        lane = lax.broadcasted_iota(jnp.int32, (per, out_rows, 2 * LANES), 2)
        after = jnp.bitwise_and(lane, LANES - 1) < LANES // 2
        parts = []
        for z in (zh, zl):
            parts.append(z[pl.ds(c * per + 1, per)])
            parts.append(jnp.where(after, z[pl.ds(c * per + 2, per)], z[pl.ds(c * per, per)]))
        parts = [part.reshape(per * out_rows, 2 * LANES) for part in parts]
        x = jnp.concatenate(parts + parts[:2], axis=1)
        y = jnp.dot(x, table[...], preferred_element_type=f32)
        y = y.reshape(per, out_rows, 2 * LANES)
        return [(y[b, :, :LANES], y[b, :, LANES:]) for b in range(per)]

    def forward_a(c):
        fields = []
        for b in range(per):
            n = c * per + b
            at = slice(n * LANES, (n + 1) * LANES)
            sn, cs = sincos(jnp.concatenate([p0h[0, :, at], phase[0, :, at], p0h[1, :, at]], axis=0))
            yc, ys = ecol[0, n:n + 1, :], ecol[1, n:n + 1, :]
            tr, ti = cs * yc - sn * ys, cs * ys + sn * yc
            ec, es = erow[0], erow[1]
            re, im = tr * ec - ti * es, tr * es + ti * ec
            w0s[n, :, :LANES] = re[2 * reach:2 * reach + rows]
            w0s[n, :, LANES:] = im[2 * reach:2 * reach + rows]
            fields.append((re, im))
            sn, cs = sincos(jnp.concatenate([p1h[0, :, at], phase[1, :, at], p1h[1, :, at]], axis=0))
            t1s[n, :, :LANES] = cs * inside1
            t1s[n, :, LANES:] = sn * inside1
        rows_conv(fields, rf64, zah, zal, c)

    def forward_b(c):
        fields = []
        for b, (re, im) in enumerate(cols_conv(zah, zal, wf, c)):
            n = c * per + b
            cs, sn = t1s[n, :, :LANES], t1s[n, :, LANES:]
            wr, wi = cs * re - sn * im, cs * im + sn * re
            w1s[n, :, :LANES] = wr[reach:reach + rows]
            w1s[n, :, LANES:] = wi[reach:reach + rows]
            fields.append((wr, wi))
        rows_conv(fields, rf32, zbh, zbl, c)

    def forward_c(c):
        for b, (re, im) in enumerate(cols_conv(zbh, zbl, wf, c)):
            n = c * per + b
            at = slice(n * LANES, (n + 1) * LANES)
            lam[n, :, :LANES] = re - meas[0, 0, :, at]
            lam[n, :, LANES:] = im - meas[0, 1, :, at]

    def backward_a(c):
        fields = []
        for b in range(per):
            n = c * per + b
            x = jnp.concatenate([lamh[0, n], lam[n], lamh[1, n]], axis=0)
            fields.append((x[:, :LANES], x[:, LANES:]))
        rows_conv(fields, rb64, zch, zcl, c)

    def send_terms(k, c):
        for p in range(c * pieces_per_chunk, (c + 1) * pieces_per_chunk):
            @pl.when(q != p)
            def _():
                g_copy(k, p).start()

            @pl.when(q == p)
            def _():
                rsr[q, k] = gs[k, p * piece:(p + 1) * piece]

    def backward_b(c):
        fields = []
        for b, (re, im) in enumerate(cols_conv(zch, zcl, wb, c)):
            n = c * per + b
            own = slice(reach, reach + rows)
            gs[1, n] = w1s[n, :, :LANES] * im[own] - w1s[n, :, LANES:] * re[own]
            cs, sn = t1s[n, :, :LANES], t1s[n, :, LANES:]
            fields.append((cs * re + sn * im, cs * im - sn * re))
        rows_conv(fields, rb32, zdh, zdl, c)

    def backward_c(c):
        for b, (re, im) in enumerate(cols_conv(zdh, zdl, wb, c)):
            n = c * per + b
            gs[0, n] = w0s[n, :, :LANES] * im - w0s[n, :, LANES:] * re

    relay((0, 1))
    loads[2].wait()
    for step in range(chunks + 2):
        if step < chunks:
            arriving(lambda side: p0_copy(side, step), 0, step)
            arriving(lambda side: p1_copy(side, step), 1, step)
            forward_a(step)
        if 0 <= step - 1 < chunks:
            forward_b(step - 1)
        if step == 2:
            loads[3].wait()
        if 0 <= step - 2:
            forward_c(step - 2)
            sending(lambda side: l_copy(side, step - 2), 2, step - 2)

    relay((2,))
    for step in range(chunks + 2):
        if step < chunks:
            arriving(lambda side: l_copy(side, step), 2, step)
            backward_a(step)
        if 0 <= step - 1 < chunks:
            backward_b(step - 1)
        if 0 <= step - 2:
            backward_c(step - 2)
        if 0 <= step - 1 < chunks:
            send_terms(1, step - 1)
        if 0 <= step - 2:
            send_terms(0, step - 2)

    for k in (1, 0):
        for j in range(n_angle):
            @pl.when(q != j)
            def _():
                g_arrival(k, j).wait_recv()
        total = rsr[0, k]
        for j in range(1, n_angle):
            total = total + rsr[j, k]
        for b in range(piece):
            out[k, :, b * LANES:(b + 1) * LANES] = total[b]

    for c in range(chunks):
        sent(lambda side: p0_copy(side, c), 0, c)
        sent(lambda side: p1_copy(side, c), 1, c)
        sent(lambda side: l_copy(side, c), 2, c)
    for k in (0, 1):
        for p in range(n_angle):
            @pl.when(q != p)
            def _():
                g_copy(k, p).wait_send()


def body(n_space, n_angle, phase_delay, measured, tilts, fresnel_taps):
    slices, rows, cols = phase_delay.shape
    reach = (fresnel_taps.shape[2] - 1) // 2
    blocks = cols // LANES
    chunks = 4
    wide, widest = rows + 2 * reach, rows + 4 * reach
    piece = blocks // n_angle
    vmem = pltpu.VMEM
    dma = pltpu.SemaphoreType.DMA
    scratch = [
        vmem((slices, rows, cols), f32), vmem((1, 2, rows, cols), f32),
        pltpu.SMEM(tilts.shape, f32), pltpu.SMEM(fresnel_taps.shape, f32),
        vmem((2, rows, cols), f32), vmem((2, reach, cols), f32),
        vmem((2, widest, LANES), f32), vmem((2, blocks, LANES), f32),
        vmem((blocks, wide, 2 * LANES), f32),
        vmem((blocks, rows, 2 * LANES), f32), vmem((blocks, rows, 2 * LANES), f32),
    ]
    for height in (wide, rows, wide, rows):
        scratch += [vmem((blocks + 2, height, 2 * LANES), bf16)] * 2
    scratch += [
        vmem((6 * 256, 256), bf16), vmem((6 * 256, 256), bf16),
        vmem((4 * wide, widest), bf16), vmem((4 * rows, wide), bf16),
        vmem((4 * wide, widest), bf16), vmem((4 * rows, wide), bf16),
        vmem((blocks, rows, 2 * LANES), f32), vmem((2, blocks, rows, 2 * LANES), f32),
        vmem((2, blocks, rows, LANES), f32), vmem((n_angle, 2, piece, rows, LANES), f32),
    ]
    scratch += [dma((2, chunks))] * 6 + [dma((2, n_angle))] * 2 + [dma((4,))]
    scratch += [
        vmem((2, rows, cols // 2), f32), vmem((2, reach, cols // 2), f32),
        vmem((2, blocks // 2, rows, 2 * LANES), f32),
    ] + [dma((3, 2, chunks))] * 4
    in_hbm = pl.BlockSpec(memory_space=pltpu.HBM)
    return pl.pallas_call(
        functools.partial(kernel, (n_space, n_angle, chunks)),
        out_shape=jax.ShapeDtypeStruct((slices, rows, cols // n_angle), f32),
        in_specs=[in_hbm] * 4,
        out_specs=pl.BlockSpec(memory_space=pltpu.VMEM),
        scratch_shapes=scratch,
        compiler_params=pltpu.CompilerParams(
            collective_id=0, has_side_effects=True, vmem_limit_bytes=62 * 1024 * 1024),
    )(phase_delay, measured, tilts, fresnel_taps)


def solution(mesh):
    return jax.shard_map(
        functools.partial(body, mesh.shape["space"], mesh.shape["angle"]),
        mesh=mesh,
        in_specs=(P(None, "space", None), P("angle", None, "space", None), P("angle", None), P()),
        out_specs=P(None, "space", "angle"),
        check_vma=False,
    )
```

```python
import functools

import jax
import jax.numpy as jnp
from jax import lax
from jax.experimental import pallas as pl
from jax.experimental.pallas import tpu as pltpu
from jax.sharding import PartitionSpec as P

LANES = 128
MESH = pl.DeviceIdType.MESH
f32 = jnp.float32
bf16 = jnp.bfloat16


def sincos(x):
    k = jnp.floor(x * f32(0.3183098861837907) + f32(0.5))
    r = ((x - k * f32(3.140625)) - k * f32(9.67502593994140625e-4)) - k * f32(1.509957990978376e-7)
    sign = f32(1.0) - f32(2.0) * (k - f32(2.0) * jnp.floor(k * f32(0.5)))
    z = r * r
    s = f32(-2.5052108e-8)
    for c in (2.7557319e-6, -1.9841270e-4, 8.3333333e-3, -1.6666667e-1, 1.0):
        s = s * z + f32(c)
    c_ = f32(2.0876757e-9)
    for c in (-2.7557319e-7, 2.4801587e-5, -1.3888889e-3, 4.1666667e-2, -0.5, 1.0):
        c_ = c_ * z + f32(c)
    return sign * s * r, sign * c_


def phase_sincos(x):
    z = x * x
    s = f32(9.984293181e-12)
    for k in (-1.209355185e-08, 8.137806969e-06, -2.604165700e-03, 2.499999993e-01):
        s = s * z + f32(k)
    s = s * x
    c = f32(3.553096396e-10)
    for k in (-3.383580022e-07, 1.627510656e-04, -3.124995776e-02, 9.999999694e-01):
        c = c * z + f32(k)
    for _ in range(2):
        d = s + s
        s, c = d * c, f32(1.0) - d * s
    return s, c


def split(x):
    hi = x.astype(bf16)
    return hi, (x - hi.astype(f32)).astype(bf16)


def kernel(
    sizes, phase_in, meas_in, tilts_in, taps_in, out, phase, meas, tilts, taps,
    p0h, p1h, erow, ecol, t1s, w0s, w1s, zah, zal, zbh, zbl, zch, zcl, zdh, zdl,
    wf, wb, rf64, rf32, rb64, rb32, lam, lamh, gs, rsr,
    p0_send, p0_recv, p1_send, p1_recv, l_send, l_recv, g_send, g_recv, load,
):
    n_space, n_angle, chunks = sizes
    rows, cols = phase.shape[1], phase.shape[2]
    n_taps = taps.shape[2]
    reach = (n_taps - 1) // 2
    wide = rows + 2 * reach
    widest = rows + 4 * reach
    blocks = cols // LANES
    per = blocks // chunks
    piece = blocks // n_angle
    pieces_per_chunk = n_angle // chunks
    width = per * LANES
    s = lax.axis_index("space")
    q = lax.axis_index("angle")
    has_up = s > 0
    has_dn = s < n_space - 1
    up_id = (jnp.maximum(s - 1, 0), q)
    dn_id = (jnp.minimum(s + 1, n_space - 1), q)

    loads = [pltpu.make_async_copy(a, b, load.at[i]) for i, (a, b) in enumerate(
        ((taps_in, taps), (tilts_in, tilts), (phase_in, phase), (meas_in, meas)))]
    for copy in loads:
        copy.start()

    barrier = pltpu.get_barrier_semaphore()

    @pl.when(has_up)
    def _():
        pl.semaphore_signal(barrier, inc=1, device_id=up_id, device_id_type=MESH)

    @pl.when(has_dn)
    def _():
        pl.semaphore_signal(barrier, inc=1, device_id=dn_id, device_id_type=MESH)

    for j in range(n_angle):
        @pl.when(q != j)
        def _():
            pl.semaphore_signal(barrier, inc=1, device_id=(s, jnp.int32(j)), device_id_type=MESH)

    expected = n_angle - 1 + jnp.where(has_up, 1, 0) + jnp.where(has_dn, 1, 0)
    pl.semaphore_wait(barrier, expected)

    def p0_copy(side, c):
        at = pl.ds(c * width, width)
        return pltpu.make_async_remote_copy(
            phase_in.at[0, :, at], p0h.at[side, :, at], p0_send.at[side, c], p0_recv.at[side, c],
            device_id=dn_id if side == 0 else up_id, device_id_type=MESH)

    def p1_copy(side, c):
        at = pl.ds(c * width, width)
        first = rows - reach if side == 0 else 0
        return pltpu.make_async_remote_copy(
            phase_in.at[1, pl.ds(first, reach), at], p1h.at[side, :, at], p1_send.at[side, c], p1_recv.at[side, c],
            device_id=dn_id if side == 0 else up_id, device_id_type=MESH)

    def l_copy(side, c):
        at = pl.ds(c * per, per)
        return pltpu.make_async_remote_copy(
            lam.at[at], lamh.at[side, at], l_send.at[side, c], l_recv.at[side, c],
            device_id=dn_id if side == 0 else up_id, device_id_type=MESH)

    def g_copy(k, p):
        return pltpu.make_async_remote_copy(
            gs.at[k, pl.ds(p * piece, piece)], rsr.at[q, k], g_send.at[k, p], g_recv.at[k, q],
            device_id=(s, jnp.int32(p)), device_id_type=MESH)

    def g_arrival(k, j):
        return pltpu.make_async_remote_copy(
            gs.at[k, pl.ds(0, piece)], rsr.at[j, k], g_send.at[k, 0], g_recv.at[k, j],
            device_id=(s, jnp.int32(j)), device_id_type=MESH)

    def sending(make):
        @pl.when(has_dn)
        def _():
            make(0).start()

        @pl.when(has_up)
        def _():
            make(1).start()

    def arriving(make):
        @pl.when(has_up)
        def _():
            make(0).wait_recv()

        @pl.when(has_dn)
        def _():
            make(1).wait_recv()

    def sent(make):
        @pl.when(has_dn)
        def _():
            make(0).wait_send()

        @pl.when(has_up)
        def _():
            make(1).wait_send()

    for c in range(chunks):
        sending(lambda side: p0_copy(side, c))
        sending(lambda side: p1_copy(side, c))

    @pl.when(jnp.logical_not(has_up))
    def _():
        p0h[0] = jnp.zeros(p0h.shape[1:], f32)
        p1h[0] = jnp.zeros(p1h.shape[1:], f32)
        lamh[0] = jnp.zeros(lamh.shape[1:], f32)

    @pl.when(jnp.logical_not(has_dn))
    def _():
        p0h[1] = jnp.zeros(p0h.shape[1:], f32)
        p1h[1] = jnp.zeros(p1h.shape[1:], f32)
        lamh[1] = jnp.zeros(lamh.shape[1:], f32)

    for ref in (zah, zal, zbh, zbl, zch, zcl, zdh, zdl):
        ref[0] = jnp.zeros(ref.shape[1:], bf16)
        ref[blocks + 1] = jnp.zeros(ref.shape[1:], bf16)

    loads[0].wait()
    group = 8
    first = lax.broadcasted_iota(jnp.int32, (group, LANES), 0)
    lane8 = lax.broadcasted_iota(jnp.int32, (group, LANES), 1)
    turn = jnp.bitwise_and(lane8 - first + LANES, LANES - 1)
    r_turn = jnp.bitwise_and(first + reach - lane8 + LANES, LANES - 1)
    base = [jnp.zeros((group, LANES), f32)] * 8
    for step in range(n_taps):
        a = step - reach
        hr, hi = taps[1, 0, step], taps[1, 1, step]
        gr, gi = taps[0, 0, step], taps[0, 1, step]
        hits = (turn == a % LANES, turn == -a % LANES, r_turn == a % LANES, r_turn == -a % LANES)
        values = (hr, hi, hr, -hi, gr, gi, gr, -gi)
        base = [jnp.where(hits[i // 2], values[i], base[i]) for i in range(8)]

    def circulant(x, count):
        return jnp.concatenate(
            [x] + [pltpu.roll(x, group * i, 1) for i in range(1, count // group)], axis=0)

    cr, ci, br, bi = [circulant(x, LANES) for x in base[:4]]
    rr, ri, ar, ai = [circulant(x, wide) for x in base[4:]]
    away = (lax.broadcasted_iota(jnp.int32, (LANES, LANES), 1)
            - lax.broadcasted_iota(jnp.int32, (LANES, LANES), 0))
    near = jnp.abs(away) <= reach
    masks = (near, jnp.abs(away) >= LANES - reach)
    for table, real, imag in ((wf, cr, ci), (wb, br, bi)):
        for m, mask in enumerate(masks):
            re, im = jnp.where(mask, real, 0.0), jnp.where(mask, imag, 0.0)
            hi, lo = split(jnp.concatenate(
                [jnp.concatenate([re, im], axis=1), jnp.concatenate([-im, re], axis=1)], axis=0))
            table[pl.ds(256 * m, 256)] = hi
            table[pl.ds(256 * (m + 2), 256)] = hi
            table[pl.ds(256 * (m + 4), 256)] = lo
    for big, small, real, imag in ((rf64, rf32, rr, ri), (rb64, rb32, ar, ai)):
        for table, out_rows, depth in ((big, wide, widest), (small, rows, wide)):
            re, im = real[:out_rows, :depth], imag[:out_rows, :depth]
            hi, lo = split(jnp.concatenate(
                [jnp.concatenate([re, -im], axis=1), jnp.concatenate([im, re], axis=1)], axis=0))
            table[:, :2 * depth] = hi
            table[:, 2 * depth:4 * depth] = hi
            table[:, 4 * depth:] = lo

    loads[1].wait()
    row_at = lax.broadcasted_iota(jnp.int32, (widest, LANES), 0)
    row_no = (s * rows - 2 * reach + row_at).astype(f32)
    es, ec = sincos(tilts[0, 0] * row_no)
    inside = jnp.where(row_at < 2 * reach, jnp.where(has_up, 1.0, 0.0),
                       jnp.where(row_at >= 2 * reach + rows, jnp.where(has_dn, 1.0, 0.0), 1.0)).astype(f32)
    erow[0] = ec * inside
    erow[1] = es * inside
    w_at = lax.broadcasted_iota(jnp.int32, (wide, LANES), 0)
    inside1 = jnp.where(w_at < reach, jnp.where(has_up, 1.0, 0.0),
                        jnp.where(w_at >= reach + rows, jnp.where(has_dn, 1.0, 0.0), 1.0)).astype(f32)
    col_no = (lax.broadcasted_iota(jnp.int32, (blocks, LANES), 0) * LANES
              + lax.broadcasted_iota(jnp.int32, (blocks, LANES), 1)).astype(f32)
    ys, yc = sincos(tilts[0, 1] * col_no)
    ecol[0] = yc
    ecol[1] = ys

    def rows_conv(fields, matrix, zh, zl, c):
        out_rows = matrix.shape[0] // 2
        hi, lo = split(jnp.concatenate([jnp.concatenate(part, axis=1) for part in zip(*fields)], axis=0))
        y = jnp.dot(matrix[...], jnp.concatenate([hi, lo, hi], axis=0), preferred_element_type=f32)
        for b in range(per):
            at = slice(b * LANES, (b + 1) * LANES)
            h, l = split(jnp.concatenate([y[:out_rows, at], y[out_rows:, at]], axis=1))
            zh[1 + c * per + b] = h
            zl[1 + c * per + b] = l

    def cols_conv(zh, zl, table, c):
        out_rows = zh.shape[1]
        lane = lax.broadcasted_iota(jnp.int32, (per, out_rows, 2 * LANES), 2)
        after = jnp.bitwise_and(lane, LANES - 1) < LANES // 2
        parts = []
        for z in (zh, zl):
            parts.append(z[pl.ds(c * per + 1, per)])
            parts.append(jnp.where(after, z[pl.ds(c * per + 2, per)], z[pl.ds(c * per, per)]))
        parts = [part.reshape(per * out_rows, 2 * LANES) for part in parts]
        x = jnp.concatenate(parts + parts[:2], axis=1)
        y = jnp.dot(x, table[...], preferred_element_type=f32)
        y = y.reshape(per, out_rows, 2 * LANES)
        return [(y[b, :, :LANES], y[b, :, LANES:]) for b in range(per)]

    def forward_a(c):
        fields = []
        for b in range(per):
            n = c * per + b
            at = slice(n * LANES, (n + 1) * LANES)
            sn, cs = phase_sincos(jnp.concatenate([p0h[0, :, at], phase[0, :, at], p0h[1, :, at]], axis=0))
            yc, ys = ecol[0, n:n + 1, :], ecol[1, n:n + 1, :]
            tr, ti = cs * yc - sn * ys, cs * ys + sn * yc
            ec, es = erow[0], erow[1]
            re, im = tr * ec - ti * es, tr * es + ti * ec
            w0s[n, :, :LANES] = re[2 * reach:2 * reach + rows]
            w0s[n, :, LANES:] = im[2 * reach:2 * reach + rows]
            fields.append((re, im))
            sn, cs = phase_sincos(jnp.concatenate([p1h[0, :, at], phase[1, :, at], p1h[1, :, at]], axis=0))
            t1s[n, :, :LANES] = cs * inside1
            t1s[n, :, LANES:] = sn * inside1
        rows_conv(fields, rf64, zah, zal, c)

    def forward_b(c):
        fields = []
        for b, (re, im) in enumerate(cols_conv(zah, zal, wf, c)):
            n = c * per + b
            cs, sn = t1s[n, :, :LANES], t1s[n, :, LANES:]
            wr, wi = cs * re - sn * im, cs * im + sn * re
            w1s[n, :, :LANES] = wr[reach:reach + rows]
            w1s[n, :, LANES:] = wi[reach:reach + rows]
            fields.append((wr, wi))
        rows_conv(fields, rf32, zbh, zbl, c)

    def forward_c(c):
        for b, (re, im) in enumerate(cols_conv(zbh, zbl, wf, c)):
            n = c * per + b
            at = slice(n * LANES, (n + 1) * LANES)
            lam[n, :, :LANES] = re - meas[0, 0, :, at]
            lam[n, :, LANES:] = im - meas[0, 1, :, at]

    def backward_a(c):
        fields = []
        for b in range(per):
            n = c * per + b
            x = jnp.concatenate([lamh[0, n], lam[n], lamh[1, n]], axis=0)
            fields.append((x[:, :LANES], x[:, LANES:]))
        rows_conv(fields, rb64, zch, zcl, c)

    def send_terms(k, c):
        for p in range(c * pieces_per_chunk, (c + 1) * pieces_per_chunk):
            @pl.when(q != p)
            def _():
                g_copy(k, p).start()

            @pl.when(q == p)
            def _():
                rsr[q, k] = gs[k, p * piece:(p + 1) * piece]

    def backward_b(c):
        fields = []
        for b, (re, im) in enumerate(cols_conv(zch, zcl, wb, c)):
            n = c * per + b
            own = slice(reach, reach + rows)
            gs[1, n] = w1s[n, :, :LANES] * im[own] - w1s[n, :, LANES:] * re[own]
            cs, sn = t1s[n, :, :LANES], t1s[n, :, LANES:]
            fields.append((cs * re + sn * im, cs * im - sn * re))
        rows_conv(fields, rb32, zdh, zdl, c)

    def backward_c(c):
        for b, (re, im) in enumerate(cols_conv(zdh, zdl, wb, c)):
            n = c * per + b
            gs[0, n] = w0s[n, :, :LANES] * im - w0s[n, :, LANES:] * re

    loads[2].wait()
    for step in range(chunks + 2):
        if step < chunks:
            arriving(lambda side: p0_copy(side, step))
            arriving(lambda side: p1_copy(side, step))
            forward_a(step)
        if 0 <= step - 1 < chunks:
            forward_b(step - 1)
        if step == 2:
            loads[3].wait()
        if 0 <= step - 2:
            forward_c(step - 2)
            sending(lambda side: l_copy(side, step - 2))

    for step in range(chunks + 2):
        if step < chunks:
            arriving(lambda side: l_copy(side, step))
            backward_a(step)
        if 0 <= step - 1 < chunks:
            backward_b(step - 1)
        if 0 <= step - 2:
            backward_c(step - 2)
        if 0 <= step - 1 < chunks:
            send_terms(1, step - 1)
        if 0 <= step - 2:
            send_terms(0, step - 2)

    for k in (1, 0):
        for j in range(n_angle):
            @pl.when(q != j)
            def _():
                g_arrival(k, j).wait_recv()
        total = rsr[0, k]
        for j in range(1, n_angle):
            total = total + rsr[j, k]
        for b in range(piece):
            out[k, :, b * LANES:(b + 1) * LANES] = total[b]

    for c in range(chunks):
        sent(lambda side: p0_copy(side, c))
        sent(lambda side: p1_copy(side, c))
        sent(lambda side: l_copy(side, c))
    for k in (0, 1):
        for p in range(n_angle):
            @pl.when(q != p)
            def _():
                g_copy(k, p).wait_send()


def body(n_space, n_angle, phase_delay, measured, tilts, fresnel_taps):
    slices, rows, cols = phase_delay.shape
    reach = (fresnel_taps.shape[2] - 1) // 2
    blocks = cols // LANES
    chunks = 4
    wide, widest = rows + 2 * reach, rows + 4 * reach
    piece = blocks // n_angle
    vmem = pltpu.VMEM
    dma = pltpu.SemaphoreType.DMA
    scratch = [
        vmem((slices, rows, cols), f32), vmem((1, 2, rows, cols), f32),
        pltpu.SMEM(tilts.shape, f32), pltpu.SMEM(fresnel_taps.shape, f32),
        vmem((2, rows, cols), f32), vmem((2, reach, cols), f32),
        vmem((2, widest, LANES), f32), vmem((2, blocks, LANES), f32),
        vmem((blocks, wide, 2 * LANES), f32),
        vmem((blocks, rows, 2 * LANES), f32), vmem((blocks, rows, 2 * LANES), f32),
    ]
    for height in (wide, rows, wide, rows):
        scratch += [vmem((blocks + 2, height, 2 * LANES), bf16)] * 2
    scratch += [
        vmem((6 * 256, 256), bf16), vmem((6 * 256, 256), bf16),
        vmem((2 * wide, 6 * widest), bf16), vmem((2 * rows, 6 * wide), bf16),
        vmem((2 * wide, 6 * widest), bf16), vmem((2 * rows, 6 * wide), bf16),
        vmem((blocks, rows, 2 * LANES), f32), vmem((2, blocks, rows, 2 * LANES), f32),
        vmem((2, blocks, rows, LANES), f32), vmem((n_angle, 2, piece, rows, LANES), f32),
    ]
    scratch += [dma((2, chunks))] * 6 + [dma((2, n_angle))] * 2 + [dma((4,))]
    in_hbm = pl.BlockSpec(memory_space=pltpu.HBM)
    return pl.pallas_call(
        functools.partial(kernel, (n_space, n_angle, chunks)),
        out_shape=jax.ShapeDtypeStruct((slices, rows, cols // n_angle), f32),
        in_specs=[in_hbm] * 4,
        out_specs=pl.BlockSpec(memory_space=pltpu.VMEM),
        scratch_shapes=scratch,
        compiler_params=pltpu.CompilerParams(
            collective_id=0, has_side_effects=True, vmem_limit_bytes=62 * 1024 * 1024),
    )(phase_delay, measured, tilts, fresnel_taps)


def solution(mesh):
    return jax.shard_map(
        functools.partial(body, mesh.shape["space"], mesh.shape["angle"]),
        mesh=mesh,
        in_specs=(P(None, "space", None), P("angle", None, "space", None), P("angle", None), P()),
        out_specs=P(None, "space", "angle"),
        check_vma=False,
    )
```

```python
import functools

import jax
import jax.numpy as jnp
from jax import lax
from jax.experimental import pallas as pl
from jax.experimental.pallas import tpu as pltpu
from jax.sharding import PartitionSpec as P

LANES = 128
MESH = pl.DeviceIdType.MESH
f32 = jnp.float32
bf16 = jnp.bfloat16


def sincos(x):
    k = jnp.floor(x * f32(0.3183098861837907) + f32(0.5))
    r = ((x - k * f32(3.140625)) - k * f32(9.67502593994140625e-4)) - k * f32(1.509957990978376e-7)
    sign = f32(1.0) - f32(2.0) * (k - f32(2.0) * jnp.floor(k * f32(0.5)))
    z = r * r
    s = f32(-2.5052108e-8)
    for c in (2.7557319e-6, -1.9841270e-4, 8.3333333e-3, -1.6666667e-1, 1.0):
        s = s * z + f32(c)
    c_ = f32(2.0876757e-9)
    for c in (-2.7557319e-7, 2.4801587e-5, -1.3888889e-3, 4.1666667e-2, -0.5, 1.0):
        c_ = c_ * z + f32(c)
    return sign * s * r, sign * c_


def phase_sincos(x):
    z = x * x
    s = f32(9.984293181e-12)
    for k in (-1.209355185e-08, 8.137806969e-06, -2.604165700e-03, 2.499999993e-01):
        s = s * z + f32(k)
    s = s * x
    c = f32(3.553096396e-10)
    for k in (-3.383580022e-07, 1.627510656e-04, -3.124995776e-02, 9.999999694e-01):
        c = c * z + f32(k)
    for _ in range(2):
        d = s + s
        s, c = d * c, f32(1.0) - d * s
    return s, c


def lanes_at(start, size):
    return pl.ds(start if isinstance(start, int) else pl.multiple_of(start, LANES), size)


def split(x):
    hi = x.astype(bf16)
    return hi, (x - hi.astype(f32)).astype(bf16)


def kernel(
    sizes, phase_in, meas_in, tilts_in, taps_in, out, phase, meas, tilts, taps,
    p0h, p1h, erow, ecol, t1s, w0s, w1s, zah, zal, zbh, zbl, zch, zcl, zdh, zdl,
    wf, wb, rf64, rf32, rb64, rb32, lam, lamh, gs, rsr,
    p0_send, p0_recv, p1_send, p1_recv, l_send, l_recv, g_send, g_recv, load,
):
    n_space, n_angle, chunks = sizes
    rows, cols = phase.shape[1], phase.shape[2]
    n_taps = taps.shape[2]
    reach = (n_taps - 1) // 2
    wide = rows + 2 * reach
    widest = rows + 4 * reach
    blocks = cols // LANES
    per = blocks // chunks
    piece = blocks // n_angle
    pieces_per_chunk = n_angle // chunks
    width = per * LANES
    s = lax.axis_index("space")
    q = lax.axis_index("angle")
    has_up = s > 0
    has_dn = s < n_space - 1
    up_id = (jnp.maximum(s - 1, 0), q)
    dn_id = (jnp.minimum(s + 1, n_space - 1), q)

    loads = [pltpu.make_async_copy(a, b, load.at[i]) for i, (a, b) in enumerate(
        ((taps_in, taps), (tilts_in, tilts), (phase_in, phase), (meas_in, meas)))]
    for copy in loads:
        copy.start()

    barrier = pltpu.get_barrier_semaphore()

    @pl.when(has_up)
    def _():
        pl.semaphore_signal(barrier, inc=1, device_id=up_id, device_id_type=MESH)

    @pl.when(has_dn)
    def _():
        pl.semaphore_signal(barrier, inc=1, device_id=dn_id, device_id_type=MESH)

    for j in range(n_angle):
        @pl.when(q != j)
        def _():
            pl.semaphore_signal(barrier, inc=1, device_id=(s, jnp.int32(j)), device_id_type=MESH)

    expected = n_angle - 1 + jnp.where(has_up, 1, 0) + jnp.where(has_dn, 1, 0)
    pl.semaphore_wait(barrier, expected)

    def p0_copy(side, c):
        at = lanes_at(c * width, width)
        return pltpu.make_async_remote_copy(
            phase_in.at[0, :, at], p0h.at[side, :, at], p0_send.at[side, c], p0_recv.at[side, c],
            device_id=dn_id if side == 0 else up_id, device_id_type=MESH)

    def p1_copy(side, c):
        at = lanes_at(c * width, width)
        first = rows - reach if side == 0 else 0
        return pltpu.make_async_remote_copy(
            phase_in.at[1, pl.ds(first, reach), at], p1h.at[side, :, at], p1_send.at[side, c], p1_recv.at[side, c],
            device_id=dn_id if side == 0 else up_id, device_id_type=MESH)

    def l_copy(side, c):
        at = pl.ds(c * per, per)
        return pltpu.make_async_remote_copy(
            lam.at[at], lamh.at[side, at], l_send.at[side, c], l_recv.at[side, c],
            device_id=dn_id if side == 0 else up_id, device_id_type=MESH)

    def g_copy(k, p):
        return pltpu.make_async_remote_copy(
            gs.at[k, pl.ds(p * piece, piece)], rsr.at[q, k], g_send.at[k, p], g_recv.at[k, q],
            device_id=(s, jnp.int32(p)), device_id_type=MESH)

    def g_arrival(k, j):
        return pltpu.make_async_remote_copy(
            gs.at[k, pl.ds(0, piece)], rsr.at[j, k], g_send.at[k, 0], g_recv.at[k, j],
            device_id=(s, jnp.int32(j)), device_id_type=MESH)

    def sending(make):
        @pl.when(has_dn)
        def _():
            make(0).start()

        @pl.when(has_up)
        def _():
            make(1).start()

    def arriving(make):
        @pl.when(has_up)
        def _():
            make(0).wait_recv()

        @pl.when(has_dn)
        def _():
            make(1).wait_recv()

    def sent(make):
        @pl.when(has_dn)
        def _():
            make(0).wait_send()

        @pl.when(has_up)
        def _():
            make(1).wait_send()

    def turn_of(step):
        return jnp.where(q < n_angle // 2, chunks - 1 - step, step)

    for step in range(chunks):
        c = turn_of(step)
        sending(lambda side: p0_copy(side, c))
        sending(lambda side: p1_copy(side, c))

    @pl.when(jnp.logical_not(has_up))
    def _():
        p0h[0] = jnp.zeros(p0h.shape[1:], f32)
        p1h[0] = jnp.zeros(p1h.shape[1:], f32)
        lamh[0] = jnp.zeros(lamh.shape[1:], f32)

    @pl.when(jnp.logical_not(has_dn))
    def _():
        p0h[1] = jnp.zeros(p0h.shape[1:], f32)
        p1h[1] = jnp.zeros(p1h.shape[1:], f32)
        lamh[1] = jnp.zeros(lamh.shape[1:], f32)

    for ref in (zah, zal, zbh, zbl, zch, zcl, zdh, zdl):
        ref[0] = jnp.zeros(ref.shape[1:], bf16)
        ref[blocks + 1] = jnp.zeros(ref.shape[1:], bf16)

    loads[0].wait()
    group = 8
    first = lax.broadcasted_iota(jnp.int32, (group, LANES), 0)
    lane8 = lax.broadcasted_iota(jnp.int32, (group, LANES), 1)
    turn = jnp.bitwise_and(lane8 - first + LANES, LANES - 1)
    r_turn = jnp.bitwise_and(first + reach - lane8 + LANES, LANES - 1)
    base = [jnp.zeros((group, LANES), f32)] * 8
    for step in range(n_taps):
        a = step - reach
        hr, hi = taps[1, 0, step], taps[1, 1, step]
        gr, gi = taps[0, 0, step], taps[0, 1, step]
        hits = (turn == a % LANES, turn == -a % LANES, r_turn == a % LANES, r_turn == -a % LANES)
        values = (hr, hi, hr, -hi, gr, gi, gr, -gi)
        base = [jnp.where(hits[i // 2], values[i], base[i]) for i in range(8)]

    def circulant(x, count):
        return jnp.concatenate(
            [x] + [pltpu.roll(x, group * i, 1) for i in range(1, count // group)], axis=0)

    cr, ci, br, bi = [circulant(x, LANES) for x in base[:4]]
    rr, ri, ar, ai = [circulant(x, wide) for x in base[4:]]
    away = (lax.broadcasted_iota(jnp.int32, (LANES, LANES), 1)
            - lax.broadcasted_iota(jnp.int32, (LANES, LANES), 0))
    near = jnp.abs(away) <= reach
    masks = (near, jnp.abs(away) >= LANES - reach)
    for table, real, imag in ((wf, cr, ci), (wb, br, bi)):
        for m, mask in enumerate(masks):
            re, im = jnp.where(mask, real, 0.0), jnp.where(mask, imag, 0.0)
            hi, lo = split(jnp.concatenate(
                [jnp.concatenate([re, im], axis=1), jnp.concatenate([-im, re], axis=1)], axis=0))
            table[pl.ds(256 * m, 256)] = hi
            table[pl.ds(256 * (m + 2), 256)] = hi
            table[pl.ds(256 * (m + 4), 256)] = lo
    for big, small, real, imag in ((rf64, rf32, rr, ri), (rb64, rb32, ar, ai)):
        for table, out_rows, depth in ((big, wide, widest), (small, rows, wide)):
            re, im = real[:out_rows, :depth], imag[:out_rows, :depth]
            hi, lo = split(jnp.concatenate(
                [jnp.concatenate([re, -im], axis=1), jnp.concatenate([im, re], axis=1)], axis=0))
            table[:, :2 * depth] = hi
            table[:, 2 * depth:4 * depth] = hi
            table[:, 4 * depth:] = lo

    loads[1].wait()
    row_at = lax.broadcasted_iota(jnp.int32, (widest, LANES), 0)
    row_no = (s * rows - 2 * reach + row_at).astype(f32)
    es, ec = sincos(tilts[0, 0] * row_no)
    inside = jnp.where(row_at < 2 * reach, jnp.where(has_up, 1.0, 0.0),
                       jnp.where(row_at >= 2 * reach + rows, jnp.where(has_dn, 1.0, 0.0), 1.0)).astype(f32)
    erow[0] = ec * inside
    erow[1] = es * inside
    w_at = lax.broadcasted_iota(jnp.int32, (wide, LANES), 0)
    inside1 = jnp.where(w_at < reach, jnp.where(has_up, 1.0, 0.0),
                        jnp.where(w_at >= reach + rows, jnp.where(has_dn, 1.0, 0.0), 1.0)).astype(f32)
    col_no = (lax.broadcasted_iota(jnp.int32, (blocks, LANES), 0) * LANES
              + lax.broadcasted_iota(jnp.int32, (blocks, LANES), 1)).astype(f32)
    ys, yc = sincos(tilts[0, 1] * col_no)
    ecol[0] = yc
    ecol[1] = ys

    def rows_conv(fields, matrix, zh, zl, c):
        out_rows = matrix.shape[0] // 2
        hi, lo = split(jnp.concatenate([jnp.concatenate(part, axis=1) for part in zip(*fields)], axis=0))
        y = jnp.dot(matrix[...], jnp.concatenate([hi, lo, hi], axis=0), preferred_element_type=f32)
        for b in range(per):
            at = slice(b * LANES, (b + 1) * LANES)
            h, l = split(jnp.concatenate([y[:out_rows, at], y[out_rows:, at]], axis=1))
            zh[1 + c * per + b] = h
            zl[1 + c * per + b] = l

    def cols_conv(zh, zl, table, c):
        out_rows = zh.shape[1]
        lane = lax.broadcasted_iota(jnp.int32, (per, out_rows, 2 * LANES), 2)
        after = jnp.bitwise_and(lane, LANES - 1) < LANES // 2
        parts = []
        for z in (zh, zl):
            parts.append(z[pl.ds(c * per + 1, per)])
            parts.append(jnp.where(after, z[pl.ds(c * per + 2, per)], z[pl.ds(c * per, per)]))
        parts = [part.reshape(per * out_rows, 2 * LANES) for part in parts]
        x = jnp.concatenate(parts + parts[:2], axis=1)
        y = jnp.dot(x, table[...], preferred_element_type=f32)
        y = y.reshape(per, out_rows, 2 * LANES)
        return [(y[b, :, :LANES], y[b, :, LANES:]) for b in range(per)]

    def forward_a(c):
        fields = []
        for b in range(per):
            n = c * per + b
            at = lanes_at(n * LANES, LANES)
            sn, cs = phase_sincos(jnp.concatenate([p0h[0, :, at], phase[0, :, at], p0h[1, :, at]], axis=0))
            yc, ys = ecol[0, pl.ds(n, 1), :], ecol[1, pl.ds(n, 1), :]
            tr, ti = cs * yc - sn * ys, cs * ys + sn * yc
            ec, es = erow[0], erow[1]
            re, im = tr * ec - ti * es, tr * es + ti * ec
            w0s[n, :, :LANES] = re[2 * reach:2 * reach + rows]
            w0s[n, :, LANES:] = im[2 * reach:2 * reach + rows]
            fields.append((re, im))
            sn, cs = phase_sincos(jnp.concatenate([p1h[0, :, at], phase[1, :, at], p1h[1, :, at]], axis=0))
            t1s[n, :, :LANES] = cs * inside1
            t1s[n, :, LANES:] = sn * inside1
        rows_conv(fields, rf64, zah, zal, c)

    def forward_b(c):
        fields = []
        for b, (re, im) in enumerate(cols_conv(zah, zal, wf, c)):
            n = c * per + b
            cs, sn = t1s[n, :, :LANES], t1s[n, :, LANES:]
            wr, wi = cs * re - sn * im, cs * im + sn * re
            w1s[n, :, :LANES] = wr[reach:reach + rows]
            w1s[n, :, LANES:] = wi[reach:reach + rows]
            fields.append((wr, wi))
        rows_conv(fields, rf32, zbh, zbl, c)

    def forward_c(c):
        for b, (re, im) in enumerate(cols_conv(zbh, zbl, wf, c)):
            n = c * per + b
            at = lanes_at(n * LANES, LANES)
            lam[n, :, :LANES] = re - meas[0, 0, :, at]
            lam[n, :, LANES:] = im - meas[0, 1, :, at]

    def backward_a(c):
        fields = []
        for b in range(per):
            n = c * per + b
            x = jnp.concatenate([lamh[0, n], lam[n], lamh[1, n]], axis=0)
            fields.append((x[:, :LANES], x[:, LANES:]))
        rows_conv(fields, rb64, zch, zcl, c)

    def send_terms(k, c):
        for i in range(pieces_per_chunk):
            p = c * pieces_per_chunk + i

            @pl.when(q != p)
            def _():
                g_copy(k, p).start()

            @pl.when(q == p)
            def _():
                rsr[q, k] = gs[k, pl.ds(p * piece, piece)]

    def backward_b(c):
        fields = []
        for b, (re, im) in enumerate(cols_conv(zch, zcl, wb, c)):
            n = c * per + b
            own = slice(reach, reach + rows)
            gs[1, n] = w1s[n, :, :LANES] * im[own] - w1s[n, :, LANES:] * re[own]
            cs, sn = t1s[n, :, :LANES], t1s[n, :, LANES:]
            fields.append((cs * re + sn * im, cs * im - sn * re))
        rows_conv(fields, rb32, zdh, zdl, c)

    def backward_c(c):
        for b, (re, im) in enumerate(cols_conv(zdh, zdl, wb, c)):
            n = c * per + b
            gs[0, n] = w0s[n, :, :LANES] * im - w0s[n, :, LANES:] * re

    loads[2].wait()
    order = [turn_of(step) for step in range(chunks)]
    for step in range(chunks + 2):
        if step < chunks:
            c = order[step]
            arriving(lambda side: p0_copy(side, c))
            arriving(lambda side: p1_copy(side, c))
            forward_a(c)
        if 0 <= step - 1 < chunks:
            forward_b(order[step - 1])
        if step == 2:
            loads[3].wait()
        if 0 <= step - 2:
            c = order[step - 2]
            forward_c(c)
            sending(lambda side: l_copy(side, c))

    for step in range(chunks + 2):
        if step < chunks:
            c = order[step]
            arriving(lambda side: l_copy(side, c))
            backward_a(c)
        if 0 <= step - 1 < chunks:
            backward_b(order[step - 1])
        if 0 <= step - 2:
            backward_c(order[step - 2])
        if 0 <= step - 1 < chunks:
            send_terms(1, order[step - 1])
        if 0 <= step - 2:
            send_terms(0, order[step - 2])

    for k in (1, 0):
        for j in range(n_angle):
            @pl.when(q != j)
            def _():
                g_arrival(k, j).wait_recv()
        total = rsr[0, k]
        for j in range(1, n_angle):
            total = total + rsr[j, k]
        for b in range(piece):
            out[k, :, b * LANES:(b + 1) * LANES] = total[b]

    for c in range(chunks):
        sent(lambda side: p0_copy(side, c))
        sent(lambda side: p1_copy(side, c))
        sent(lambda side: l_copy(side, c))
    for k in (0, 1):
        for p in range(n_angle):
            @pl.when(q != p)
            def _():
                g_copy(k, p).wait_send()


def body(n_space, n_angle, phase_delay, measured, tilts, fresnel_taps):
    slices, rows, cols = phase_delay.shape
    reach = (fresnel_taps.shape[2] - 1) // 2
    blocks = cols // LANES
    chunks = 4
    wide, widest = rows + 2 * reach, rows + 4 * reach
    piece = blocks // n_angle
    vmem = pltpu.VMEM
    dma = pltpu.SemaphoreType.DMA
    scratch = [
        vmem((slices, rows, cols), f32), vmem((1, 2, rows, cols), f32),
        pltpu.SMEM(tilts.shape, f32), pltpu.SMEM(fresnel_taps.shape, f32),
        vmem((2, rows, cols), f32), vmem((2, reach, cols), f32),
        vmem((2, widest, LANES), f32), vmem((2, blocks, LANES), f32),
        vmem((blocks, wide, 2 * LANES), f32),
        vmem((blocks, rows, 2 * LANES), f32), vmem((blocks, rows, 2 * LANES), f32),
    ]
    for height in (wide, rows, wide, rows):
        scratch += [vmem((blocks + 2, height, 2 * LANES), bf16)] * 2
    scratch += [
        vmem((6 * 256, 256), bf16), vmem((6 * 256, 256), bf16),
        vmem((2 * wide, 6 * widest), bf16), vmem((2 * rows, 6 * wide), bf16),
        vmem((2 * wide, 6 * widest), bf16), vmem((2 * rows, 6 * wide), bf16),
        vmem((blocks, rows, 2 * LANES), f32), vmem((2, blocks, rows, 2 * LANES), f32),
        vmem((2, blocks, rows, LANES), f32), vmem((n_angle, 2, piece, rows, LANES), f32),
    ]
    scratch += [dma((2, chunks))] * 6 + [dma((2, n_angle))] * 2 + [dma((4,))]
    in_hbm = pl.BlockSpec(memory_space=pltpu.HBM)
    return pl.pallas_call(
        functools.partial(kernel, (n_space, n_angle, chunks)),
        out_shape=jax.ShapeDtypeStruct((slices, rows, cols // n_angle), f32),
        in_specs=[in_hbm] * 4,
        out_specs=pl.BlockSpec(memory_space=pltpu.VMEM),
        scratch_shapes=scratch,
        compiler_params=pltpu.CompilerParams(
            collective_id=0, has_side_effects=True, vmem_limit_bytes=62 * 1024 * 1024),
    )(phase_delay, measured, tilts, fresnel_taps)


def solution(mesh):
    return jax.shard_map(
        functools.partial(body, mesh.shape["space"], mesh.shape["angle"]),
        mesh=mesh,
        in_specs=(P(None, "space", None), P("angle", None, "space", None), P("angle", None), P()),
        out_specs=P(None, "space", "angle"),
        check_vma=False,
    )
```

```python
import functools

import jax
import jax.numpy as jnp
from jax import lax
from jax.experimental import pallas as pl
from jax.experimental.pallas import tpu as pltpu
from jax.sharding import PartitionSpec as P

LANES = 128
MESH = pl.DeviceIdType.MESH
f32 = jnp.float32
bf16 = jnp.bfloat16


def sincos(x):
    k = jnp.floor(x * f32(0.3183098861837907) + f32(0.5))
    r = ((x - k * f32(3.140625)) - k * f32(9.67502593994140625e-4)) - k * f32(1.509957990978376e-7)
    sign = f32(1.0) - f32(2.0) * (k - f32(2.0) * jnp.floor(k * f32(0.5)))
    z = r * r
    s = f32(-2.5052108e-8)
    for c in (2.7557319e-6, -1.9841270e-4, 8.3333333e-3, -1.6666667e-1, 1.0):
        s = s * z + f32(c)
    c_ = f32(2.0876757e-9)
    for c in (-2.7557319e-7, 2.4801587e-5, -1.3888889e-3, 4.1666667e-2, -0.5, 1.0):
        c_ = c_ * z + f32(c)
    return sign * s * r, sign * c_


def phase_sincos(x):
    z = x * x
    s = f32(9.984293181e-12)
    for k in (-1.209355185e-08, 8.137806969e-06, -2.604165700e-03, 2.499999993e-01):
        s = s * z + f32(k)
    s = s * x
    c = f32(3.553096396e-10)
    for k in (-3.383580022e-07, 1.627510656e-04, -3.124995776e-02, 9.999999694e-01):
        c = c * z + f32(k)
    for _ in range(2):
        d = s + s
        s, c = d * c, f32(1.0) - d * s
    return s, c


def lanes_at(start, size):
    return pl.ds(start if isinstance(start, int) else pl.multiple_of(start, LANES), size)


def split(x):
    hi = x.astype(bf16)
    return hi, (x - hi.astype(f32)).astype(bf16)


def kernel(
    sizes, phase_in, meas_in, tilts_in, taps_in, out, phase, meas, tilts, taps,
    p0h, p1h, erow, ecol, t1s, w0s, w1s, zah, zal, zbh, zbl, zch, zcl, zdh, zdl,
    wf, wb, rf64, rf32, rb64, rb32, lam, lamh, gs, rsr,
    p0_send, p0_recv, p1_send, p1_recv, l_send, l_recv, g_send, g_recv, load,
    acc, acc_send, acc_recv,
):
    n_space, n_angle, chunks = sizes
    rows, cols = phase.shape[1], phase.shape[2]
    n_taps = taps.shape[2]
    reach = (n_taps - 1) // 2
    wide = rows + 2 * reach
    widest = rows + 4 * reach
    blocks = cols // LANES
    per = blocks // chunks
    piece = blocks // n_angle
    pieces_per_chunk = n_angle // chunks
    width = per * LANES
    s = lax.axis_index("space")
    q = lax.axis_index("angle")
    has_up = s > 0
    has_dn = s < n_space - 1
    up_id = (jnp.maximum(s - 1, 0), q)
    dn_id = (jnp.minimum(s + 1, n_space - 1), q)

    loads = [pltpu.make_async_copy(a, b, load.at[i]) for i, (a, b) in enumerate(
        ((taps_in, taps), (tilts_in, tilts), (phase_in, phase), (meas_in, meas)))]
    for copy in loads:
        copy.start()

    barrier = pltpu.get_barrier_semaphore()

    @pl.when(has_up)
    def _():
        pl.semaphore_signal(barrier, inc=1, device_id=up_id, device_id_type=MESH)

    @pl.when(has_dn)
    def _():
        pl.semaphore_signal(barrier, inc=1, device_id=dn_id, device_id_type=MESH)

    for j in range(n_angle):
        @pl.when(q != j)
        def _():
            pl.semaphore_signal(barrier, inc=1, device_id=(s, jnp.int32(j)), device_id_type=MESH)

    expected = n_angle - 1 + jnp.where(has_up, 1, 0) + jnp.where(has_dn, 1, 0)
    pl.semaphore_wait(barrier, expected)

    def p0_copy(side, c):
        at = lanes_at(c * width, width)
        return pltpu.make_async_remote_copy(
            phase_in.at[0, :, at], p0h.at[side, :, at], p0_send.at[side, c], p0_recv.at[side, c],
            device_id=dn_id if side == 0 else up_id, device_id_type=MESH)

    def p1_copy(side, c):
        at = lanes_at(c * width, width)
        first = rows - reach if side == 0 else 0
        return pltpu.make_async_remote_copy(
            phase_in.at[1, pl.ds(first, reach), at], p1h.at[side, :, at], p1_send.at[side, c], p1_recv.at[side, c],
            device_id=dn_id if side == 0 else up_id, device_id_type=MESH)

    def l_copy(side, c):
        at = pl.ds(c * per, per)
        return pltpu.make_async_remote_copy(
            lam.at[at], lamh.at[side, at], l_send.at[side, c], l_recv.at[side, c],
            device_id=dn_id if side == 0 else up_id, device_id_type=MESH)

    def g_copy(k, p):
        return pltpu.make_async_remote_copy(
            gs.at[k, pl.ds(p * piece, piece)], rsr.at[q, k], g_send.at[k, p], g_recv.at[k, q],
            device_id=(s, jnp.int32(p)), device_id_type=MESH)

    def g_arrival(k, j):
        return pltpu.make_async_remote_copy(
            gs.at[k, pl.ds(0, piece)], rsr.at[j, k], g_send.at[k, 0], g_recv.at[k, j],
            device_id=(s, jnp.int32(j)), device_id_type=MESH)

    paired = n_angle == 4 and chunks == 4
    inner = (q > 0) & (q < n_angle - 1)
    partner = q + 1 - 2 * lax.rem(q, 2)

    def to_partner(k, p):
        slot = lax.rem(p, 2)
        return pltpu.make_async_remote_copy(
            gs.at[k, pl.ds(p * piece, piece)], acc.at[k, slot], acc_send.at[k, slot], acc_recv.at[k, slot],
            device_id=(s, partner), device_id_type=MESH)

    def sending(make):
        @pl.when(has_dn)
        def _():
            make(0).start()

        @pl.when(has_up)
        def _():
            make(1).start()

    def arriving(make):
        @pl.when(has_up)
        def _():
            make(0).wait_recv()

        @pl.when(has_dn)
        def _():
            make(1).wait_recv()

    def sent(make):
        @pl.when(has_dn)
        def _():
            make(0).wait_send()

        @pl.when(has_up)
        def _():
            make(1).wait_send()

    def turn_of(step):
        return jnp.where(q < n_angle // 2, chunks - 1 - step, step)

    order = [turn_of(step) for step in range(chunks)]
    for c in order:
        sending(lambda side: p0_copy(side, c))
        sending(lambda side: p1_copy(side, c))

    @pl.when(jnp.logical_not(has_up))
    def _():
        p0h[0] = jnp.zeros(p0h.shape[1:], f32)
        p1h[0] = jnp.zeros(p1h.shape[1:], f32)
        lamh[0] = jnp.zeros(lamh.shape[1:], f32)

    @pl.when(jnp.logical_not(has_dn))
    def _():
        p0h[1] = jnp.zeros(p0h.shape[1:], f32)
        p1h[1] = jnp.zeros(p1h.shape[1:], f32)
        lamh[1] = jnp.zeros(lamh.shape[1:], f32)

    for ref in (zah, zal, zbh, zbl, zch, zcl, zdh, zdl):
        ref[0] = jnp.zeros(ref.shape[1:], bf16)
        ref[blocks + 1] = jnp.zeros(ref.shape[1:], bf16)

    loads[0].wait()
    group = 8
    first = lax.broadcasted_iota(jnp.int32, (group, LANES), 0)
    lane8 = lax.broadcasted_iota(jnp.int32, (group, LANES), 1)
    turn = jnp.bitwise_and(lane8 - first + LANES, LANES - 1)
    r_turn = jnp.bitwise_and(first + reach - lane8 + LANES, LANES - 1)
    base = [jnp.zeros((group, LANES), f32)] * 8
    for step in range(n_taps):
        a = step - reach
        hr, hi = taps[1, 0, step], taps[1, 1, step]
        gr, gi = taps[0, 0, step], taps[0, 1, step]
        hits = (turn == a % LANES, turn == -a % LANES, r_turn == a % LANES, r_turn == -a % LANES)
        values = (hr, hi, hr, -hi, gr, gi, gr, -gi)
        base = [jnp.where(hits[i // 2], values[i], base[i]) for i in range(8)]

    def circulant(x, count):
        return jnp.concatenate(
            [x] + [pltpu.roll(x, group * i, 1) for i in range(1, count // group)], axis=0)

    cr, ci, br, bi = [circulant(x, LANES) for x in base[:4]]
    rr, ri, ar, ai = [circulant(x, wide) for x in base[4:]]
    away = (lax.broadcasted_iota(jnp.int32, (LANES, LANES), 1)
            - lax.broadcasted_iota(jnp.int32, (LANES, LANES), 0))
    near = jnp.abs(away) <= reach
    masks = (near, jnp.abs(away) >= LANES - reach)
    for table, real, imag in ((wf, cr, ci), (wb, br, bi)):
        for m, mask in enumerate(masks):
            re, im = jnp.where(mask, real, 0.0), jnp.where(mask, imag, 0.0)
            hi, lo = split(jnp.concatenate(
                [jnp.concatenate([re, im], axis=1), jnp.concatenate([-im, re], axis=1)], axis=0))
            table[pl.ds(256 * m, 256)] = hi
            table[pl.ds(256 * (m + 2), 256)] = hi
            table[pl.ds(256 * (m + 4), 256)] = lo
    for big, small, real, imag in ((rf64, rf32, rr, ri), (rb64, rb32, ar, ai)):
        for table, out_rows, depth in ((big, wide, widest), (small, rows, wide)):
            re, im = real[:out_rows, :depth], imag[:out_rows, :depth]
            hi, lo = split(jnp.concatenate(
                [jnp.concatenate([re, -im], axis=1), jnp.concatenate([im, re], axis=1)], axis=0))
            table[:, :2 * depth] = hi
            table[:, 2 * depth:4 * depth] = hi
            table[:, 4 * depth:] = lo

    loads[1].wait()
    row_at = lax.broadcasted_iota(jnp.int32, (widest, LANES), 0)
    row_no = (s * rows - 2 * reach + row_at).astype(f32)
    es, ec = sincos(tilts[0, 0] * row_no)
    inside = jnp.where(row_at < 2 * reach, jnp.where(has_up, 1.0, 0.0),
                       jnp.where(row_at >= 2 * reach + rows, jnp.where(has_dn, 1.0, 0.0), 1.0)).astype(f32)
    erow[0] = ec * inside
    erow[1] = es * inside
    w_at = lax.broadcasted_iota(jnp.int32, (wide, LANES), 0)
    inside1 = jnp.where(w_at < reach, jnp.where(has_up, 1.0, 0.0),
                        jnp.where(w_at >= reach + rows, jnp.where(has_dn, 1.0, 0.0), 1.0)).astype(f32)
    col_no = (lax.broadcasted_iota(jnp.int32, (blocks, LANES), 0) * LANES
              + lax.broadcasted_iota(jnp.int32, (blocks, LANES), 1)).astype(f32)
    ys, yc = sincos(tilts[0, 1] * col_no)
    ecol[0] = yc
    ecol[1] = ys

    def rows_conv(fields, matrix, zh, zl, c):
        out_rows = matrix.shape[0] // 2
        hi, lo = split(jnp.concatenate([jnp.concatenate(part, axis=1) for part in zip(*fields)], axis=0))
        y = jnp.dot(matrix[...], jnp.concatenate([hi, lo, hi], axis=0), preferred_element_type=f32)
        for b in range(per):
            at = slice(b * LANES, (b + 1) * LANES)
            h, l = split(jnp.concatenate([y[:out_rows, at], y[out_rows:, at]], axis=1))
            zh[1 + c * per + b] = h
            zl[1 + c * per + b] = l

    def cols_conv(zh, zl, table, c):
        out_rows = zh.shape[1]
        lane = lax.broadcasted_iota(jnp.int32, (per, out_rows, 2 * LANES), 2)
        after = jnp.bitwise_and(lane, LANES - 1) < LANES // 2
        parts = []
        for z in (zh, zl):
            parts.append(z[pl.ds(c * per + 1, per)])
            parts.append(jnp.where(after, z[pl.ds(c * per + 2, per)], z[pl.ds(c * per, per)]))
        parts = [part.reshape(per * out_rows, 2 * LANES) for part in parts]
        x = jnp.concatenate(parts + parts[:2], axis=1)
        y = jnp.dot(x, table[...], preferred_element_type=f32)
        y = y.reshape(per, out_rows, 2 * LANES)
        return [(y[b, :, :LANES], y[b, :, LANES:]) for b in range(per)]

    def forward_a(c):
        fields = []
        for b in range(per):
            n = c * per + b
            at = lanes_at(n * LANES, LANES)
            sn, cs = phase_sincos(jnp.concatenate([p0h[0, :, at], phase[0, :, at], p0h[1, :, at]], axis=0))
            yc, ys = ecol[0, pl.ds(n, 1), :], ecol[1, pl.ds(n, 1), :]
            tr, ti = cs * yc - sn * ys, cs * ys + sn * yc
            ec, es = erow[0], erow[1]
            re, im = tr * ec - ti * es, tr * es + ti * ec
            w0s[n, :, :LANES] = re[2 * reach:2 * reach + rows]
            w0s[n, :, LANES:] = im[2 * reach:2 * reach + rows]
            fields.append((re, im))
            sn, cs = phase_sincos(jnp.concatenate([p1h[0, :, at], phase[1, :, at], p1h[1, :, at]], axis=0))
            t1s[n, :, :LANES] = cs * inside1
            t1s[n, :, LANES:] = sn * inside1
        rows_conv(fields, rf64, zah, zal, c)

    def forward_b(c):
        fields = []
        for b, (re, im) in enumerate(cols_conv(zah, zal, wf, c)):
            n = c * per + b
            cs, sn = t1s[n, :, :LANES], t1s[n, :, LANES:]
            wr, wi = cs * re - sn * im, cs * im + sn * re
            w1s[n, :, :LANES] = wr[reach:reach + rows]
            w1s[n, :, LANES:] = wi[reach:reach + rows]
            fields.append((wr, wi))
        rows_conv(fields, rf32, zbh, zbl, c)

    def forward_c(c):
        for b, (re, im) in enumerate(cols_conv(zbh, zbl, wf, c)):
            n = c * per + b
            at = lanes_at(n * LANES, LANES)
            lam[n, :, :LANES] = re - meas[0, 0, :, at]
            lam[n, :, LANES:] = im - meas[0, 1, :, at]

    def backward_a(c):
        fields = []
        for b in range(per):
            n = c * per + b
            x = jnp.concatenate([lamh[0, n], lam[n], lamh[1, n]], axis=0)
            fields.append((x[:, :LANES], x[:, LANES:]))
        rows_conv(fields, rb64, zch, zcl, c)

    def send_on(k, c):
        @pl.when(inner)
        def _():
            to_partner(k, c).wait_recv()
            at = pl.ds(c * piece, piece)
            gs[k, at] = gs[k, at] + acc[k, lax.rem(c, 2)]
            g_copy(k, c).start()

    def send_terms(k, step):
        c = order[step]
        if paired and step < 2:
            @pl.when(jnp.logical_not(inner))
            def _():
                to_partner(k, c).start()

            return
        for i in range(pieces_per_chunk):
            p = c * pieces_per_chunk + i

            @pl.when(q != p)
            def _():
                g_copy(k, p).start()

            @pl.when(q == p)
            def _():
                rsr[q, k] = gs[k, pl.ds(p * piece, piece)]

    def backward_b(c):
        fields = []
        for b, (re, im) in enumerate(cols_conv(zch, zcl, wb, c)):
            n = c * per + b
            own = slice(reach, reach + rows)
            gs[1, n] = w1s[n, :, :LANES] * im[own] - w1s[n, :, LANES:] * re[own]
            cs, sn = t1s[n, :, :LANES], t1s[n, :, LANES:]
            fields.append((cs * re + sn * im, cs * im - sn * re))
        rows_conv(fields, rb32, zdh, zdl, c)

    def backward_c(c):
        for b, (re, im) in enumerate(cols_conv(zdh, zdl, wb, c)):
            n = c * per + b
            gs[0, n] = w0s[n, :, :LANES] * im - w0s[n, :, LANES:] * re

    loads[2].wait()
    for step in range(chunks + 2):
        if step < chunks:
            c = order[step]
            arriving(lambda side: p0_copy(side, c))
            arriving(lambda side: p1_copy(side, c))
            forward_a(c)
        if 0 <= step - 1 < chunks:
            forward_b(order[step - 1])
        if step == 2:
            loads[3].wait()
        if 0 <= step - 2:
            c = order[step - 2]
            forward_c(c)
            sending(lambda side: l_copy(side, c))

    for step in range(chunks + 2):
        if step < chunks:
            c = order[step]
            arriving(lambda side: l_copy(side, c))
            backward_a(c)
        if 0 <= step - 1 < chunks:
            backward_b(order[step - 1])
        if 0 <= step - 2:
            backward_c(order[step - 2])
        if 0 <= step - 1 < chunks:
            send_terms(1, step - 1)
        if 0 <= step - 2:
            send_terms(0, step - 2)
        if paired and 0 <= step - 2 < 2:
            send_on(1, order[step - 2])
        if paired and 0 <= step - 3 < 2:
            send_on(0, order[step - 3])

    for k in (1, 0):
        if paired:
            across = jnp.where(q < 2, 2, 1)
            g_arrival(k, partner).wait_recv()
            g_arrival(k, across).wait_recv()
            total = rsr[q, k] + rsr[partner, k] + rsr[across, k]
        else:
            for j in range(n_angle):
                @pl.when(q != j)
                def _():
                    g_arrival(k, j).wait_recv()
            total = rsr[0, k]
            for j in range(1, n_angle):
                total = total + rsr[j, k]
        for b in range(piece):
            out[k, :, b * LANES:(b + 1) * LANES] = total[b]

    for c in range(chunks):
        sent(lambda side: p0_copy(side, c))
        sent(lambda side: p1_copy(side, c))
        sent(lambda side: l_copy(side, c))
    for k in (0, 1):
        for p in range(n_angle):
            if paired:
                far = (q < 2) if p >= 2 else (q >= 2)
                by_hand = far & jnp.logical_not(inner)

                @pl.when(by_hand)
                def _():
                    to_partner(k, p).wait_send()

                direct = (q != p) & jnp.logical_not(by_hand)
            else:
                direct = q != p

            @pl.when(direct)
            def _():
                g_copy(k, p).wait_send()


def body(n_space, n_angle, phase_delay, measured, tilts, fresnel_taps):
    slices, rows, cols = phase_delay.shape
    reach = (fresnel_taps.shape[2] - 1) // 2
    blocks = cols // LANES
    chunks = 4
    wide, widest = rows + 2 * reach, rows + 4 * reach
    piece = blocks // n_angle
    vmem = pltpu.VMEM
    dma = pltpu.SemaphoreType.DMA
    scratch = [
        vmem((slices, rows, cols), f32), vmem((1, 2, rows, cols), f32),
        pltpu.SMEM(tilts.shape, f32), pltpu.SMEM(fresnel_taps.shape, f32),
        vmem((2, rows, cols), f32), vmem((2, reach, cols), f32),
        vmem((2, widest, LANES), f32), vmem((2, blocks, LANES), f32),
        vmem((blocks, wide, 2 * LANES), f32),
        vmem((blocks, rows, 2 * LANES), f32), vmem((blocks, rows, 2 * LANES), f32),
    ]
    for height in (wide, rows, wide, rows):
        scratch += [vmem((blocks + 2, height, 2 * LANES), bf16)] * 2
    scratch += [
        vmem((6 * 256, 256), bf16), vmem((6 * 256, 256), bf16),
        vmem((2 * wide, 6 * widest), bf16), vmem((2 * rows, 6 * wide), bf16),
        vmem((2 * wide, 6 * widest), bf16), vmem((2 * rows, 6 * wide), bf16),
        vmem((blocks, rows, 2 * LANES), f32), vmem((2, blocks, rows, 2 * LANES), f32),
        vmem((2, blocks, rows, LANES), f32), vmem((n_angle, 2, piece, rows, LANES), f32),
    ]
    scratch += [dma((2, chunks))] * 6 + [dma((2, n_angle))] * 2 + [dma((4,))]
    scratch += [vmem((2, 2, piece, rows, LANES), f32), dma((2, 2)), dma((2, 2))]
    in_hbm = pl.BlockSpec(memory_space=pltpu.HBM)
    return pl.pallas_call(
        functools.partial(kernel, (n_space, n_angle, chunks)),
        out_shape=jax.ShapeDtypeStruct((slices, rows, cols // n_angle), f32),
        in_specs=[in_hbm] * 4,
        out_specs=pl.BlockSpec(memory_space=pltpu.VMEM),
        scratch_shapes=scratch,
        compiler_params=pltpu.CompilerParams(
            collective_id=0, has_side_effects=True, vmem_limit_bytes=62 * 1024 * 1024),
    )(phase_delay, measured, tilts, fresnel_taps)


def solution(mesh):
    return jax.shard_map(
        functools.partial(body, mesh.shape["space"], mesh.shape["angle"]),
        mesh=mesh,
        in_specs=(P(None, "space", None), P("angle", None, "space", None), P("angle", None), P()),
        out_specs=P(None, "space", "angle"),
        check_vma=False,
    )
```

```python
import functools

import jax
import jax.numpy as jnp
from jax import lax
from jax.experimental import pallas as pl
from jax.experimental.pallas import tpu as pltpu
from jax.sharding import PartitionSpec as P

LANES = 128
MESH = pl.DeviceIdType.MESH
f32 = jnp.float32
bf16 = jnp.bfloat16


def sincos(x):
    k = jnp.floor(x * f32(0.3183098861837907) + f32(0.5))
    r = ((x - k * f32(3.140625)) - k * f32(9.67502593994140625e-4)) - k * f32(1.509957990978376e-7)
    sign = f32(1.0) - f32(2.0) * (k - f32(2.0) * jnp.floor(k * f32(0.5)))
    z = r * r
    s = f32(-2.5052108e-8)
    for c in (2.7557319e-6, -1.9841270e-4, 8.3333333e-3, -1.6666667e-1, 1.0):
        s = s * z + f32(c)
    c_ = f32(2.0876757e-9)
    for c in (-2.7557319e-7, 2.4801587e-5, -1.3888889e-3, 4.1666667e-2, -0.5, 1.0):
        c_ = c_ * z + f32(c)
    return sign * s * r, sign * c_


def phase_sincos(x):
    z = x * x
    s = f32(9.984293181e-12)
    for k in (-1.209355185e-08, 8.137806969e-06, -2.604165700e-03, 2.499999993e-01):
        s = s * z + f32(k)
    s = s * x
    c = f32(3.553096396e-10)
    for k in (-3.383580022e-07, 1.627510656e-04, -3.124995776e-02, 9.999999694e-01):
        c = c * z + f32(k)
    for _ in range(2):
        d = s + s
        s, c = d * c, f32(1.0) - d * s
    return s, c


def lanes_at(start, size):
    return pl.ds(start if isinstance(start, int) else pl.multiple_of(start, LANES), size)


def split(x):
    hi = x.astype(bf16)
    return hi, (x - hi.astype(f32)).astype(bf16)


def kernel(
    sizes, phase_in, meas_in, tilts_in, taps_in, out, phase, meas, tilts, taps,
    p0h, p1h, erow, ecol, t1s, w0s, w1s, zah, zal, zbh, zbl, zch, zcl, zdh, zdl,
    wf, wb, rf64, rf32, rb64, rb32, lam, lamh, gs, rsr,
    p0_send, p0_recv, p1_send, p1_recv, l_send, l_recv, g_send, g_recv, load,
):
    n_space, n_angle, chunks = sizes
    rows, cols = phase.shape[1], phase.shape[2]
    n_taps = taps.shape[2]
    reach = (n_taps - 1) // 2
    wide = rows + 2 * reach
    widest = rows + 4 * reach
    blocks = cols // LANES
    per = blocks // chunks
    piece = blocks // n_angle
    pieces_per_chunk = n_angle // chunks
    width = per * LANES
    s = lax.axis_index("space")
    q = lax.axis_index("angle")
    has_up = s > 0
    has_dn = s < n_space - 1
    up_id = (jnp.maximum(s - 1, 0), q)
    dn_id = (jnp.minimum(s + 1, n_space - 1), q)

    loads = [pltpu.make_async_copy(a, b, load.at[i]) for i, (a, b) in enumerate(
        ((taps_in, taps), (tilts_in, tilts), (phase_in, phase), (meas_in, meas)))]
    for copy in loads:
        copy.start()

    barrier = pltpu.get_barrier_semaphore()

    @pl.when(has_up)
    def _():
        pl.semaphore_signal(barrier, inc=1, device_id=up_id, device_id_type=MESH)

    @pl.when(has_dn)
    def _():
        pl.semaphore_signal(barrier, inc=1, device_id=dn_id, device_id_type=MESH)

    for j in range(n_angle):
        @pl.when(q != j)
        def _():
            pl.semaphore_signal(barrier, inc=1, device_id=(s, jnp.int32(j)), device_id_type=MESH)

    expected = n_angle - 1 + jnp.where(has_up, 1, 0) + jnp.where(has_dn, 1, 0)
    pl.semaphore_wait(barrier, expected)

    def p0_copy(side, c):
        at = lanes_at(c * width, width)
        return pltpu.make_async_remote_copy(
            phase_in.at[0, :, at], p0h.at[side, :, at], p0_send.at[side, c], p0_recv.at[side, c],
            device_id=dn_id if side == 0 else up_id, device_id_type=MESH)

    def p1_copy(side, c):
        at = lanes_at(c * width, width)
        first = rows - reach if side == 0 else 0
        return pltpu.make_async_remote_copy(
            phase_in.at[1, pl.ds(first, reach), at], p1h.at[side, :, at], p1_send.at[side, c], p1_recv.at[side, c],
            device_id=dn_id if side == 0 else up_id, device_id_type=MESH)

    def l_copy(side, c):
        at = pl.ds(c * per, per)
        return pltpu.make_async_remote_copy(
            lam.at[at], lamh.at[side, at], l_send.at[side, c], l_recv.at[side, c],
            device_id=dn_id if side == 0 else up_id, device_id_type=MESH)

    def g_copy(k, p):
        return pltpu.make_async_remote_copy(
            gs.at[k, pl.ds(p * piece, piece)], rsr.at[q, k], g_send.at[k, p], g_recv.at[k, q],
            device_id=(s, jnp.int32(p)), device_id_type=MESH)

    def g_arrival(k, j):
        return pltpu.make_async_remote_copy(
            gs.at[k, pl.ds(0, piece)], rsr.at[j, k], g_send.at[k, 0], g_recv.at[k, j],
            device_id=(s, jnp.int32(j)), device_id_type=MESH)

    def sending(make):
        @pl.when(has_dn)
        def _():
            make(0).start()

        @pl.when(has_up)
        def _():
            make(1).start()

    def arriving(make):
        @pl.when(has_up)
        def _():
            make(0).wait_recv()

        @pl.when(has_dn)
        def _():
            make(1).wait_recv()

    def sent(make):
        @pl.when(has_dn)
        def _():
            make(0).wait_send()

        @pl.when(has_up)
        def _():
            make(1).wait_send()

    def turn_of(step):
        return jnp.where(q < n_angle // 2, chunks - 1 - step, step)

    for step in range(chunks):
        c = turn_of(step)
        sending(lambda side: p0_copy(side, c))
        sending(lambda side: p1_copy(side, c))

    @pl.when(jnp.logical_not(has_up))
    def _():
        p0h[0] = jnp.zeros(p0h.shape[1:], f32)
        p1h[0] = jnp.zeros(p1h.shape[1:], f32)
        lamh[0] = jnp.zeros(lamh.shape[1:], f32)

    @pl.when(jnp.logical_not(has_dn))
    def _():
        p0h[1] = jnp.zeros(p0h.shape[1:], f32)
        p1h[1] = jnp.zeros(p1h.shape[1:], f32)
        lamh[1] = jnp.zeros(lamh.shape[1:], f32)

    for ref in (zah, zal, zbh, zbl, zch, zcl, zdh, zdl):
        ref[0] = jnp.zeros(ref.shape[1:], bf16)
        ref[blocks + 1] = jnp.zeros(ref.shape[1:], bf16)

    loads[0].wait()
    group = 8
    first = lax.broadcasted_iota(jnp.int32, (group, LANES), 0)
    lane8 = lax.broadcasted_iota(jnp.int32, (group, LANES), 1)
    turn = jnp.bitwise_and(lane8 - first + LANES, LANES - 1)
    r_turn = jnp.bitwise_and(first + reach - lane8 + LANES, LANES - 1)
    base = [jnp.zeros((group, LANES), f32)] * 8
    for step in range(n_taps):
        a = step - reach
        hr, hi = taps[1, 0, step], taps[1, 1, step]
        gr, gi = taps[0, 0, step], taps[0, 1, step]
        hits = (turn == a % LANES, turn == -a % LANES, r_turn == a % LANES, r_turn == -a % LANES)
        values = (hr, hi, hr, -hi, gr, gi, gr, -gi)
        base = [jnp.where(hits[i // 2], values[i], base[i]) for i in range(8)]

    def circulant(x, count):
        return jnp.concatenate(
            [x] + [pltpu.roll(x, group * i, 1) for i in range(1, count // group)], axis=0)

    cr, ci, br, bi = [circulant(x, LANES) for x in base[:4]]
    rr, ri, ar, ai = [circulant(x, wide) for x in base[4:]]
    away = (lax.broadcasted_iota(jnp.int32, (LANES, LANES), 1)
            - lax.broadcasted_iota(jnp.int32, (LANES, LANES), 0))
    near = jnp.abs(away) <= reach
    masks = (near, jnp.abs(away) >= LANES - reach)
    for table, real, imag in ((wf, cr, ci), (wb, br, bi)):
        for m, mask in enumerate(masks):
            re, im = jnp.where(mask, real, 0.0), jnp.where(mask, imag, 0.0)
            hi, lo = split(jnp.concatenate(
                [jnp.concatenate([re, im], axis=1), jnp.concatenate([-im, re], axis=1)], axis=0))
            table[pl.ds(256 * m, 256)] = hi
            table[pl.ds(256 * (m + 2), 256)] = hi
            table[pl.ds(256 * (m + 4), 256)] = lo
    for big, small, real, imag in ((rf64, rf32, rr, ri), (rb64, rb32, ar, ai)):
        for table, out_rows, depth in ((big, wide, widest), (small, rows, wide)):
            re, im = real[:out_rows, :depth], imag[:out_rows, :depth]
            hi, lo = split(jnp.concatenate(
                [jnp.concatenate([re, -im], axis=1), jnp.concatenate([im, re], axis=1)], axis=0))
            table[:, :2 * depth] = hi
            table[:, 2 * depth:4 * depth] = hi
            table[:, 4 * depth:] = lo

    loads[1].wait()
    row_at = lax.broadcasted_iota(jnp.int32, (widest, LANES), 0)
    row_no = (s * rows - 2 * reach + row_at).astype(f32)
    es, ec = sincos(tilts[0, 0] * row_no)
    inside = jnp.where(row_at < 2 * reach, jnp.where(has_up, 1.0, 0.0),
                       jnp.where(row_at >= 2 * reach + rows, jnp.where(has_dn, 1.0, 0.0), 1.0)).astype(f32)
    erow[0] = ec * inside
    erow[1] = es * inside
    w_at = lax.broadcasted_iota(jnp.int32, (wide, LANES), 0)
    inside1 = jnp.where(w_at < reach, jnp.where(has_up, 1.0, 0.0),
                        jnp.where(w_at >= reach + rows, jnp.where(has_dn, 1.0, 0.0), 1.0)).astype(f32)
    col_no = (lax.broadcasted_iota(jnp.int32, (blocks, LANES), 0) * LANES
              + lax.broadcasted_iota(jnp.int32, (blocks, LANES), 1)).astype(f32)
    ys, yc = sincos(tilts[0, 1] * col_no)
    ecol[0] = yc
    ecol[1] = ys

    def rows_conv(fields, matrix, zh, zl, c):
        out_rows = matrix.shape[0] // 2
        hi, lo = split(jnp.concatenate([jnp.concatenate(part, axis=1) for part in zip(*fields)], axis=0))
        y = jnp.dot(matrix[...], jnp.concatenate([hi, lo, hi], axis=0), preferred_element_type=f32)
        for b in range(per):
            at = slice(b * LANES, (b + 1) * LANES)
            h, l = split(jnp.concatenate([y[:out_rows, at], y[out_rows:, at]], axis=1))
            zh[1 + c * per + b] = h
            zl[1 + c * per + b] = l

    def cols_conv(zh, zl, table, c):
        out_rows = zh.shape[1]
        lane = lax.broadcasted_iota(jnp.int32, (per, out_rows, 2 * LANES), 2)
        after = jnp.bitwise_and(lane, LANES - 1) < LANES // 2
        parts = []
        for z in (zh, zl):
            parts.append(z[pl.ds(c * per + 1, per)])
            parts.append(jnp.where(after, z[pl.ds(c * per + 2, per)], z[pl.ds(c * per, per)]))
        parts = [part.reshape(per * out_rows, 2 * LANES) for part in parts]
        x = jnp.concatenate(parts + parts[:2], axis=1)
        y = jnp.dot(x, table[...], preferred_element_type=f32)
        y = y.reshape(per, out_rows, 2 * LANES)
        return [(y[b, :, :LANES], y[b, :, LANES:]) for b in range(per)]

    def forward_a(c):
        fields = []
        for b in range(per):
            n = c * per + b
            at = lanes_at(n * LANES, LANES)
            sn, cs = phase_sincos(jnp.concatenate([p0h[0, :, at], phase[0, :, at], p0h[1, :, at]], axis=0))
            yc, ys = ecol[0, pl.ds(n, 1), :], ecol[1, pl.ds(n, 1), :]
            tr, ti = cs * yc - sn * ys, cs * ys + sn * yc
            ec, es = erow[0], erow[1]
            re, im = tr * ec - ti * es, tr * es + ti * ec
            w0s[n, :, :LANES] = re[2 * reach:2 * reach + rows]
            w0s[n, :, LANES:] = im[2 * reach:2 * reach + rows]
            fields.append((re, im))
            sn, cs = phase_sincos(jnp.concatenate([p1h[0, :, at], phase[1, :, at], p1h[1, :, at]], axis=0))
            t1s[n, :, :LANES] = cs * inside1
            t1s[n, :, LANES:] = sn * inside1
        rows_conv(fields, rf64, zah, zal, c)

    def forward_b(c):
        fields = []
        for b, (re, im) in enumerate(cols_conv(zah, zal, wf, c)):
            n = c * per + b
            cs, sn = t1s[n, :, :LANES], t1s[n, :, LANES:]
            wr, wi = cs * re - sn * im, cs * im + sn * re
            w1s[n, :, :LANES] = wr[reach:reach + rows]
            w1s[n, :, LANES:] = wi[reach:reach + rows]
            fields.append((wr, wi))
        rows_conv(fields, rf32, zbh, zbl, c)

    def forward_c(c):
        for b, (re, im) in enumerate(cols_conv(zbh, zbl, wf, c)):
            n = c * per + b
            at = lanes_at(n * LANES, LANES)
            lam[n, :, :LANES] = re - meas[0, 0, :, at]
            lam[n, :, LANES:] = im - meas[0, 1, :, at]

    def backward_a(c):
        fields = []
        for b in range(per):
            n = c * per + b
            x = jnp.concatenate([lamh[0, n], lam[n], lamh[1, n]], axis=0)
            fields.append((x[:, :LANES], x[:, LANES:]))
        rows_conv(fields, rb64, zch, zcl, c)

    def send_terms(k, c):
        for i in range(pieces_per_chunk):
            p = c * pieces_per_chunk + i

            @pl.when(q != p)
            def _():
                g_copy(k, p).start()

            @pl.when(q == p)
            def _():
                rsr[q, k] = gs[k, pl.ds(p * piece, piece)]

    def backward_b(c):
        fields = []
        for b, (re, im) in enumerate(cols_conv(zch, zcl, wb, c)):
            n = c * per + b
            own = slice(reach, reach + rows)
            gs[1, n] = w1s[n, :, :LANES] * im[own] - w1s[n, :, LANES:] * re[own]
            cs, sn = t1s[n, :, :LANES], t1s[n, :, LANES:]
            fields.append((cs * re + sn * im, cs * im - sn * re))
        rows_conv(fields, rb32, zdh, zdl, c)

    def backward_c(c):
        for b, (re, im) in enumerate(cols_conv(zdh, zdl, wb, c)):
            n = c * per + b
            gs[0, n] = w0s[n, :, :LANES] * im - w0s[n, :, LANES:] * re

    loads[2].wait()
    order = [turn_of(step) for step in range(chunks)]
    for step in range(chunks + 2):
        if step < chunks:
            c = order[step]
            arriving(lambda side: p0_copy(side, c))
            arriving(lambda side: p1_copy(side, c))
            forward_a(c)
        if 0 <= step - 1 < chunks:
            forward_b(order[step - 1])
        if step == 2:
            loads[3].wait()
        if 0 <= step - 2:
            c = order[step - 2]
            forward_c(c)
            sending(lambda side: l_copy(side, c))

    for step in range(chunks + 2):
        if step < chunks:
            c = order[step]
            arriving(lambda side: l_copy(side, c))
            backward_a(c)
        if 0 <= step - 1 < chunks:
            backward_b(order[step - 1])
        if 0 <= step - 2:
            backward_c(order[step - 2])
        if 0 <= step - 1 < chunks:
            send_terms(1, order[step - 1])
        if 0 <= step - 2:
            send_terms(0, order[step - 2])

    for k in (1, 0):
        for j in range(n_angle):
            @pl.when(q != j)
            def _():
                g_arrival(k, j).wait_recv()
        total = rsr[0, k]
        for j in range(1, n_angle):
            total = total + rsr[j, k]
        for b in range(piece):
            out[k, :, b * LANES:(b + 1) * LANES] = total[b]

    for c in range(chunks):
        sent(lambda side: p0_copy(side, c))
        sent(lambda side: p1_copy(side, c))
        sent(lambda side: l_copy(side, c))
    for k in (0, 1):
        for p in range(n_angle):
            @pl.when(q != p)
            def _():
                g_copy(k, p).wait_send()


def body(n_space, n_angle, phase_delay, measured, tilts, fresnel_taps):
    slices, rows, cols = phase_delay.shape
    reach = (fresnel_taps.shape[2] - 1) // 2
    blocks = cols // LANES
    chunks = 2
    wide, widest = rows + 2 * reach, rows + 4 * reach
    piece = blocks // n_angle
    vmem = pltpu.VMEM
    dma = pltpu.SemaphoreType.DMA
    scratch = [
        vmem((slices, rows, cols), f32), vmem((1, 2, rows, cols), f32),
        pltpu.SMEM(tilts.shape, f32), pltpu.SMEM(fresnel_taps.shape, f32),
        vmem((2, rows, cols), f32), vmem((2, reach, cols), f32),
        vmem((2, widest, LANES), f32), vmem((2, blocks, LANES), f32),
        vmem((blocks, wide, 2 * LANES), f32),
        vmem((blocks, rows, 2 * LANES), f32), vmem((blocks, rows, 2 * LANES), f32),
    ]
    for height in (wide, rows, wide, rows):
        scratch += [vmem((blocks + 2, height, 2 * LANES), bf16)] * 2
    scratch += [
        vmem((6 * 256, 256), bf16), vmem((6 * 256, 256), bf16),
        vmem((2 * wide, 6 * widest), bf16), vmem((2 * rows, 6 * wide), bf16),
        vmem((2 * wide, 6 * widest), bf16), vmem((2 * rows, 6 * wide), bf16),
        vmem((blocks, rows, 2 * LANES), f32), vmem((2, blocks, rows, 2 * LANES), f32),
        vmem((2, blocks, rows, LANES), f32), vmem((n_angle, 2, piece, rows, LANES), f32),
    ]
    scratch += [dma((2, chunks))] * 6 + [dma((2, n_angle))] * 2 + [dma((4,))]
    in_hbm = pl.BlockSpec(memory_space=pltpu.HBM)
    return pl.pallas_call(
        functools.partial(kernel, (n_space, n_angle, chunks)),
        out_shape=jax.ShapeDtypeStruct((slices, rows, cols // n_angle), f32),
        in_specs=[in_hbm] * 4,
        out_specs=pl.BlockSpec(memory_space=pltpu.VMEM),
        scratch_shapes=scratch,
        compiler_params=pltpu.CompilerParams(
            collective_id=0, has_side_effects=True, vmem_limit_bytes=62 * 1024 * 1024),
    )(phase_delay, measured, tilts, fresnel_taps)


def solution(mesh):
    return jax.shard_map(
        functools.partial(body, mesh.shape["space"], mesh.shape["angle"]),
        mesh=mesh,
        in_specs=(P(None, "space", None), P("angle", None, "space", None), P("angle", None), P()),
        out_specs=P(None, "space", "angle"),
        check_vma=False,
    )
```
